512 devices in a mesh: dp: 32 (over y, x), ctx: 16 (over z, core).
Axes of the slice: x: 4, y: 8, z: 8, core: 2. Of those that a mesh axis runs over, the one named last changes fastest.
Arguments:
- tokens: bfloat16 [65536, 2048], P(('dp', 'ctx')), parts along dimension 0, may hold values from -64 to 64
- query_weight: bfloat16 [2048, 2048], P(None, 'ctx'), may hold values from -0.125 to 0.125
- key_matrix: bfloat16 [2048, 256], replicated, may hold values from -0.125 to 0.125
- value_matrix: bfloat16 [2048, 256], replicated, may hold values from -0.125 to 0.125
- doc_lengths: int32 [512], P('dp'), parts along dimension 0, may hold values from 64 to 512, as said below
Outputs:
- attended: bfloat16 [65536, 2048], P(('dp', 'ctx')), parts along dimension 0
The draws below stay inside these ranges and needn't reach their ends.
There are 32 independent parts, one for each index of `dp`. The reference program is written for one: setup_inputs(seed, part) draws one part's arguments, and reference() takes and returns one part's arrays. A program takes and returns all parts, laid end to end along the dimension named above; an argument that names none is the same for every part. Nothing has to cross between parts.
Inputs may be any that keep to these rules, and one draw needn't show every extreme that they name: `doc_lengths`: lengths of the 16 documents packed in order into the 2048 tokens of a group; they sum to 2048 and the longest has exactly 512 tokens.
All inputs are finite; a program needn't handle non-finite values.
Results may differ from the reference program's by a relative error of at most 0.011.
Values may be sent and summed in bfloat16 or wider, within the bound.
No kernel may reach another device: no remote copies, remote signals or barrier semaphores. Data moves between devices by JAX's collectives and lax.ppermute only.
A program may use at most 64 MiB of HBM per device.

```python
import math
import jax
import jax.numpy as jnp
from jax import lax

MODEL_WIDTH = 2048
QUERY_HEADS = 16
KEY_VALUE_HEADS = 2
HEAD_SIZE = 128
NDOC = 16
TOKENS = 2048
DOC_MOST = 512
DOC_LEAST = 64


def draw_tokens(key, part):
    base = jnp.clip(jax.random.normal(key, (TOKENS, MODEL_WIDTH), jnp.float32), -6.0, 6.0)
    return base.astype(jnp.bfloat16)


def draw_doc_lengths(key, part):
    first, second = jax.random.split(jax.random.fold_in(key, 11))
    others = NDOC - 1
    spare = TOKENS - DOC_MOST - others * DOC_LEAST
    shares = jax.random.randint(first, (others,), 1, 9).astype(jnp.int32)
    cumulative = jnp.cumsum(shares).astype(jnp.int32)
    marks = spare * cumulative // cumulative[-1]
    pieces = marks - jnp.concatenate([jnp.zeros((1,), jnp.int32), marks[:-1]])
    lengths = (pieces + DOC_LEAST).astype(jnp.int32)
    place = jax.random.randint(second, (), 0, NDOC).astype(jnp.int32)
    slots = jnp.arange(NDOC, dtype=jnp.int32)
    below = jnp.take(lengths, jnp.clip(slots, 0, others - 1))
    above = jnp.take(lengths, jnp.clip(slots - 1, 0, others - 1))
    return jnp.where(slots < place, below, jnp.where(slots == place, DOC_MOST, above)).astype(jnp.int32)


def shard_levels(rng, extent, cuts, smallest, top_value):
    def one(position, blocks):
        steps = jax.random.uniform(jax.random.fold_in(jax.random.fold_in(rng, 6), position), (blocks,), jnp.float32, smallest / len(cuts), top_value / len(cuts))
        return jnp.repeat(jnp.exp(steps), extent[position] // blocks).reshape((-1,) + (1,) * (len(extent) - position - 1))

    level = one(*cuts[0])
    for cut in cuts[1:]:
        level = level * one(*cut)
    return level


def normal_values(rng, dims, scale, limit, cuts=(), kind=jnp.bfloat16):
    array = jax.random.normal(rng, dims, jnp.float32) * scale
    if len(cuts) > 0:
        array = shard_levels(rng, dims, cuts, -0.22, 0.18) * array
    return jnp.clip(array, min=-limit, max=limit).astype(kind)


def setup_inputs(seed: int = 0, part: int = 0) -> dict:
    seeds = jax.random.split(jax.random.key(seed), 6)
    part_keys = jax.random.split(jax.random.fold_in(seeds[5], part), 6)
    tokens = draw_tokens(jax.random.fold_in(jax.random.fold_in(seeds[5], part), 71), part)
    query_weight = normal_values(seeds[1], (MODEL_WIDTH, QUERY_HEADS * HEAD_SIZE), MODEL_WIDTH ** -0.5, 0.125, ((1, 16),))
    key_matrix = normal_values(seeds[2], (MODEL_WIDTH, KEY_VALUE_HEADS * HEAD_SIZE), MODEL_WIDTH ** -0.5, 0.125)
    value_matrix = normal_values(seeds[3], (MODEL_WIDTH, KEY_VALUE_HEADS * HEAD_SIZE), MODEL_WIDTH ** -0.5, 0.125)
    doc_lengths = draw_doc_lengths(jax.random.fold_in(jax.random.fold_in(seeds[5], part), 71), part)
    return {"tokens": tokens, "query_weight": query_weight, "key_matrix": key_matrix, "value_matrix": value_matrix, "doc_lengths": doc_lengths}


NEG = -1e+30

def doc_ids(doc_lengths, positions):
    ends = jnp.cumsum(doc_lengths).astype(jnp.int32)
    return lax.optimization_barrier(jnp.sum((positions[:, None] >= ends[None, :]).astype(jnp.int32), axis=1)).astype(jnp.int32)

def reference(tokens, query_weight, key_matrix, value_matrix, doc_lengths):
    running_total = tokens.shape[0]
    head_group = QUERY_HEADS // KEY_VALUE_HEADS
    query_matrix = lax.optimization_barrier(jnp.dot(tokens, query_weight, preferred_element_type=jnp.float32).astype(jnp.bfloat16))
    key_rows = lax.optimization_barrier(jnp.dot(tokens, key_matrix, preferred_element_type=jnp.float32).astype(jnp.bfloat16))
    value_rows = lax.optimization_barrier(jnp.dot(tokens, value_matrix, preferred_element_type=jnp.float32).astype(jnp.bfloat16))
    docs = doc_ids(doc_lengths, jnp.arange(running_total, dtype=jnp.int32))
    ends = jnp.cumsum(doc_lengths).astype(jnp.int32)
    starts = (ends - doc_lengths).astype(jnp.int32)
    key_rows3 = key_rows.reshape(running_total, KEY_VALUE_HEADS, HEAD_SIZE).astype(jnp.float32)
    value_rows3 = value_rows.reshape(running_total, KEY_VALUE_HEADS, HEAD_SIZE).astype(jnp.float32)
    current_block = math.gcd(running_total, 512)
    block_list = running_total // current_block
    window = min(running_total, 2 * DOC_MOST + current_block)
    query_block_list = query_matrix.reshape(block_list, current_block, KEY_VALUE_HEADS, head_group, HEAD_SIZE)
    doc_blocks = docs.reshape(block_list, current_block)
    scale = 1.0 / math.sqrt(HEAD_SIZE)
    slots = jnp.arange(NDOC, dtype=jnp.int32)

    def one_block(items):
        query_block, query_docs = items
        low = jnp.sum(jnp.where(slots == query_docs[0], starts, 0)).astype(jnp.int32)
        begin = jnp.clip(low, 0, running_total - window).astype(jnp.int32)
        key_part = lax.dynamic_slice_in_dim(key_rows3, begin, window, 0)
        value_part = lax.dynamic_slice_in_dim(value_rows3, begin, window, 0)
        key_docs = lax.dynamic_slice_in_dim(docs, begin, window, 0)
        scores = jnp.einsum('qkgd,mkd->kgqm', query_block.astype(jnp.float32), key_part) * scale
        allowed = (query_docs[:, None] == key_docs[None, :])[None, None]
        scores = jnp.where(allowed, scores, NEG)
        highest = lax.optimization_barrier(jnp.max(scores, axis=-1, keepdims=True))
        weights = jnp.where(allowed, jnp.exp(scores - highest), 0.0)
        summed = lax.optimization_barrier(jnp.sum(weights, axis=-1))
        rounded = lax.optimization_barrier(weights.astype(jnp.bfloat16)).astype(jnp.float32)
        mixed = jnp.einsum('kgqm,mkd->kgqd', rounded, value_part)
        result = (mixed / summed[..., None]).astype(jnp.bfloat16)
        return jnp.transpose(result, (2, 0, 1, 3)).reshape(current_block, QUERY_HEADS * HEAD_SIZE)
    outputs = lax.map(one_block, (query_block_list, doc_blocks))
    return outputs.reshape(running_total, QUERY_HEADS * HEAD_SIZE)
```

```python
import functools
import math

import jax
import jax.numpy as jnp
from jax import lax
from jax.experimental import pallas as pl
from jax.experimental.pallas import tpu as pltpu
from jax.sharding import PartitionSpec as P

QUERY_HEADS = 16
HEAD_SIZE = 128
WIDTH = 2048
ROWS = 128
NEG = -1e30

YS, XS, ZS, CORES = 8, 4, 8, 2
AXES = ("dp", "ctx")
ORDER = ((5, 3, 1, 7, 4, 2, 0, 6), (7, 3, 0, 6, 2, 4, 1, 5))


def flat(y, x, z, c):
    return (((y % YS) * XS + x % XS) * ZS + z % ZS) * CORES + c


def color_of(y, x, z):
    return (2 * x + 3 * y + z) % 8


def everyone():
    return [(y, x, z, c) for y in range(YS) for x in range(XS) for z in range(ZS) for c in range(CORES)]


def first_moves():
    pairs = []
    for y, x, z, c in everyone():
        head = 8 * c + ORDER[c][color_of(y, x, z)]
        pairs.append((flat(y, x, head // 2, head % 2), flat(y, x, z, c)))
    return pairs


def moves(step):
    pairs = []
    for y, x, z, c in everyone():
        dy, dx, dz = step(c)
        pairs.append((flat(y + dy, x + dx, z + dz, c), flat(y, x, z, c)))
    return pairs


def swap_cores():
    return [(flat(y, x, z, 1 - c), flat(y, x, z, c)) for y, x, z, c in everyone()]


def kv_kernel(core_ref, own_ref, other_ref, key_ref, value_ref, out_ref):
    for first, rows in ((0, own_ref), (ROWS, other_ref)):
        for column, matrix in ((0, key_ref), (HEAD_SIZE, value_ref)):
            out_ref[first : first + ROWS, column : column + HEAD_SIZE] = jnp.dot(
                rows[...], matrix[...], preferred_element_type=jnp.float32
            ).astype(jnp.bfloat16)


def kv_project(core, own, other, key_matrix, value_matrix):
    whole = pl.BlockSpec((ROWS, WIDTH), lambda i, s: (0, 0))
    mine = pl.BlockSpec((WIDTH, HEAD_SIZE), lambda i, s: (0, s[0]))
    return pl.pallas_call(
        kv_kernel,
        grid_spec=pltpu.PrefetchScalarGridSpec(
            num_scalar_prefetch=1,
            grid=(1,),
            in_specs=[whole, whole, mine, mine],
            out_specs=pl.BlockSpec((2 * ROWS, 2 * HEAD_SIZE), lambda i, s: (0, 0)),
        ),
        out_shape=jax.ShapeDtypeStruct((2 * ROWS, 2 * HEAD_SIZE), jnp.bfloat16),
        compiler_params=pltpu.CompilerParams(vmem_limit_bytes=24 * 2**20),
        cost_estimate=pl.CostEstimate(flops=2**28, bytes_accessed=2**21, transcendentals=0),
    )(core, own, other, key_matrix, value_matrix)


def head_kernel(pieces, *refs):
    slot_ref, own_ref, other_ref = refs[:3]
    weights = refs[3 : 3 + pieces]
    kv = refs[3 + pieces : 8 + pieces]
    row_docs, key_docs, held_ref, out_ref = refs[8 + pieces :]
    depth = WIDTH // pieces
    parts = []
    for rows in (own_ref, other_ref):
        total = None
        for i in range(pieces):
            term = jnp.dot(
                rows[:, i * depth : (i + 1) * depth], weights[i][...], preferred_element_type=jnp.float32
            )
            total = term if total is None else total + term
        parts.append(total.astype(jnp.bfloat16))
    queries = jnp.concatenate(parts, axis=0)
    factor = math.log2(math.e) / math.sqrt(HEAD_SIZE)
    docs = row_docs[...]
    scores = []
    for i in range(5):
        product = lax.dot_general(
            queries, kv[i][:, :HEAD_SIZE], (((1,), (1,)), ((), ())), preferred_element_type=jnp.float32
        )
        allowed = docs == key_docs[:, i * 2 * ROWS : (i + 1) * 2 * ROWS]
        scores.append(jnp.where(allowed, product, NEG))
    highest = functools.reduce(jnp.maximum, [jnp.max(s, axis=1, keepdims=True) for s in scores])
    summed, mixed = 0.0, 0.0
    for i in range(5):
        part = jnp.exp2((scores[i] - highest) * factor)
        summed = summed + jnp.sum(part, axis=1, keepdims=True)
        mixed = mixed + jnp.dot(
            part.astype(jnp.bfloat16), kv[i][:, HEAD_SIZE:], preferred_element_type=jnp.float32
        )
    out_ref[...] = (mixed / summed).astype(jnp.bfloat16)


def one_head(slot, own, other, weights, kv, row_docs, key_docs, held):
    def whole(array):
        return pl.BlockSpec(array.shape, lambda i, s: (0, 0))

    inputs = [own, other, *weights, *kv, row_docs, key_docs]
    return pl.pallas_call(
        functools.partial(head_kernel, len(weights)),
        grid_spec=pltpu.PrefetchScalarGridSpec(
            num_scalar_prefetch=1,
            grid=(1,),
            in_specs=[whole(a) for a in inputs] + [pl.BlockSpec(memory_space=pl.ANY)],
            out_specs=pl.BlockSpec((2 * ROWS, HEAD_SIZE), lambda i, s: (0, s[0])),
        ),
        out_shape=jax.ShapeDtypeStruct(held.shape, held.dtype),
        input_output_aliases={1 + len(inputs): 0},
        compiler_params=pltpu.CompilerParams(vmem_limit_bytes=32 * 2**20),
        cost_estimate=pl.CostEstimate(flops=2**28, bytes_accessed=2**21, transcendentals=2**18),
    )(slot, *inputs, held)


def join_kernel(core_ref, mine_ref, other_ref, out_ref):
    half = mine_ref.shape[1]
    core = core_ref[0]
    out_ref[:, pl.ds(pl.multiple_of(core * half, half), half)] = mine_ref[...]
    out_ref[:, pl.ds(pl.multiple_of((1 - core) * half, half), half)] = other_ref[...]


def join(core, held, arrived):
    half = held.shape[1]
    return pl.pallas_call(
        join_kernel,
        grid_spec=pltpu.PrefetchScalarGridSpec(
            num_scalar_prefetch=1,
            grid=(1,),
            in_specs=[pl.BlockSpec((ROWS, half), lambda i, s: (0, 0))] * 2,
            out_specs=pl.BlockSpec((ROWS, 2 * half), lambda i, s: (0, 0)),
        ),
        out_shape=jax.ShapeDtypeStruct((ROWS, 2 * half), held.dtype),
        compiler_params=pltpu.CompilerParams(vmem_limit_bytes=8 * 2**20),
    )(core, held, arrived)


def body(tokens, query_weight, key_matrix, value_matrix, doc_lengths):
    dp, ctx = lax.axis_index("dp"), lax.axis_index("ctx")
    y, x, z, c = dp // XS, dp % XS, ctx // CORES, ctx % CORES
    core = c.reshape(1).astype(jnp.int32)

    other = lax.ppermute(tokens, AXES, swap_cores())
    held_weight = lax.ppermute(query_weight, AXES, first_moves())
    kv = kv_project(core, tokens, other, key_matrix, value_matrix)

    around = (0, 1, -1, 2, -2)
    kv_all = [kv] + [lax.ppermute(kv, AXES, moves(lambda c, d=d: (0, 0, d))) for d in around[1:]]

    slots16 = jnp.arange(16, dtype=jnp.int32)
    ends = jnp.sum(jnp.where(slots16[:, None] <= slots16[None, :], doc_lengths[:, None], 0), axis=0)
    row = jnp.arange(2 * ROWS, dtype=jnp.int32)
    within = jnp.where(row < ROWS, row + ROWS * c, row - ROWS * c)
    key_positions = jnp.concatenate([within + 2 * ROWS * ((z + d) % ZS) for d in around])
    key_docs = jnp.sum((key_positions[None, :] >= ends[:, None]).astype(jnp.int32), axis=0, keepdims=True)
    row_docs = jnp.sum(
        ((within + 2 * ROWS * z)[:, None] >= ends[None, :]).astype(jnp.int32), axis=1, keepdims=True
    )

    half = WIDTH // 2
    low = lax.ppermute(held_weight[:half], AXES, moves(lambda c: (0, 2, 0)))
    high = lax.ppermute(held_weight[half:], AXES, moves(lambda c: (1, 0, 1) if c == 0 else (-1, 0, -1)))
    steps = ((2, (0, 1, 0)), (-2, (0, -1, 0)), (3, (1, 0, 0)), (-3, (-1, 0, 0)), (1, (0, 0, 1)), (-1, (0, 0, -1)))
    arrivals = [(0, [held_weight])]
    for shift, step in steps:
        arrivals.append((shift, [lax.ppermute(held_weight, AXES, moves(lambda c, step=step: step))]))
    arrivals.append((4, [low, high]))

    order = jnp.array(ORDER, jnp.int32)
    mine = jnp.where(c == 0, order[0], order[1])
    color = (2 * x + 3 * y + z) % 8
    held = jnp.zeros((2 * ROWS, WIDTH // 2), jnp.bfloat16)
    for shift, weights in arrivals:
        slot = lax.dynamic_slice(mine, ((color + shift) % 8,), (1,))
        held = one_head(slot, tokens, other, weights, kv_all, row_docs, key_docs, held)
    arrived = lax.ppermute(held[ROWS:], AXES, swap_cores())
    return join(core, held, arrived)


def solution(mesh):
    in_specs = (P(("dp", "ctx"), None), P(None, "ctx"), P(), P(), P("dp"))
    out_specs = P(("dp", "ctx"), None)
    return jax.shard_map(body, mesh=mesh, in_specs=in_specs, out_specs=out_specs, check_vma=False)
```

```python
import functools
import math

import jax
import jax.numpy as jnp
from jax import lax
from jax.experimental import pallas as pl
from jax.experimental.pallas import tpu as pltpu
from jax.sharding import PartitionSpec as P

HEAD_SIZE = 128
WIDTH = 2048
ROWS = 128
PAIR = 2 * ROWS
HALF = 8 * HEAD_SIZE
NEG = -1e30

YS, XS, ZS, CORES = 8, 4, 8, 2
AXES = ("dp", "ctx")
ORDER = ((5, 3, 1, 7, 4, 2, 0, 6), (7, 3, 0, 6, 2, 4, 1, 5))
AROUND = (0, 1, -1, 2, -2)
VMEM = pl.BlockSpec(memory_space=pltpu.VMEM)
SMEM = pl.BlockSpec(memory_space=pltpu.SMEM)


def flat(y, x, z, c):
    return (((y % YS) * XS + x % XS) * ZS + z % ZS) * CORES + c


def everyone():
    return [(y, x, z, c) for y in range(YS) for x in range(XS) for z in range(ZS) for c in range(CORES)]


def first_moves():
    pairs = []
    for y, x, z, c in everyone():
        head = 8 * c + ORDER[c][(2 * x + 3 * y + z) % 8]
        pairs.append((flat(y, x, head // 2, head % 2), flat(y, x, z, c)))
    return pairs


def moves(step):
    pairs = []
    for y, x, z, c in everyone():
        dy, dx, dz = step(c)
        pairs.append((flat(y + dy, x + dx, z + dz, c), flat(y, x, z, c)))
    return pairs


def swap_cores(value):
    return lax.ppermute(value, AXES, [(flat(y, x, z, 1 - c), flat(y, x, z, c)) for y, x, z, c in everyone()])


def place():
    dp, ctx = lax.axis_index("dp"), lax.axis_index("ctx")
    return dp // XS, dp % XS, ctx // CORES, ctx % CORES


def kv_rows(rows, key_ref, value_ref, c, kv_ref, first):
    mine = pl.ds(pl.multiple_of(c * HEAD_SIZE, HEAD_SIZE), HEAD_SIZE)
    for column, matrix in ((0, key_ref), (HEAD_SIZE, value_ref)):
        kv_ref[first : first + ROWS, column : column + HEAD_SIZE] = jnp.dot(
            rows[...], matrix[:, mine], preferred_element_type=jnp.float32
        ).astype(jnp.bfloat16)


def own_kv_kernel(lengths_ref, own_ref, key_ref, value_ref, kv_ref, row_docs_ref, key_docs_ref):
    y, x, z, c = place()
    kv_rows(own_ref, key_ref, value_ref, c, kv_ref, 0)

    def positions(shape, axis, block):
        row = lax.broadcasted_iota(jnp.int32, shape, axis)
        return jnp.where(row < ROWS, row + ROWS * c, row - ROWS * c) + PAIR * block

    def docs(place_in_group):
        end = 0
        total = jnp.zeros(place_in_group.shape, jnp.int32)
        for e in range(16):
            end = end + lengths_ref[e]
            total = total + (place_in_group >= end).astype(jnp.int32)
        return total

    row_docs_ref[...] = docs(positions((PAIR, 1), 0, z))
    for i, step in enumerate(AROUND):
        key_docs_ref[:, i * PAIR : (i + 1) * PAIR] = docs(positions((1, PAIR), 1, (z + step + ZS) % ZS))


def other_kv_kernel(other_ref, key_ref, value_ref, held_ref, kv_ref):
    y, x, z, c = place()
    kv_rows(other_ref, key_ref, value_ref, c, kv_ref, ROWS)


def kv_project(lengths, own, other, key_matrix, value_matrix):
    kv_shape = jax.ShapeDtypeStruct((PAIR, 2 * HEAD_SIZE), jnp.bfloat16)
    settings = dict(
        compiler_params=pltpu.CompilerParams(vmem_limit_bytes=8 * 2**20),
        cost_estimate=pl.CostEstimate(flops=2**27, bytes_accessed=2**21, transcendentals=0),
    )
    kv, row_docs, key_docs = pl.pallas_call(
        own_kv_kernel,
        in_specs=[SMEM, VMEM, VMEM, VMEM],
        out_specs=[VMEM] * 3,
        out_shape=[
            kv_shape,
            jax.ShapeDtypeStruct((PAIR, 1), jnp.int32),
            jax.ShapeDtypeStruct((1, len(AROUND) * PAIR), jnp.int32),
        ],
        **settings,
    )(lengths, own, key_matrix, value_matrix)
    kv = pl.pallas_call(
        other_kv_kernel,
        in_specs=[VMEM] * 4,
        out_specs=VMEM,
        out_shape=kv_shape,
        input_output_aliases={3: 0},
        **settings,
    )(other, key_matrix, value_matrix, kv)
    return kv, row_docs, key_docs


def head_kernel(shift, own_ref, other_ref, weight_ref, *refs):
    kv, (row_docs, key_docs, _, _, keep_ref, send_ref) = refs[:5], refs[5:]
    y, x, z, c = place()
    color = (2 * x + 3 * y + z + shift) % 8
    slot = 0
    for k in range(8):
        slot = slot + jnp.where(color == k, jnp.where(c == 0, ORDER[0][k], ORDER[1][k]), 0)
    queries = jnp.concatenate(
        [
            jnp.dot(rows[...], weight_ref[...], preferred_element_type=jnp.float32).astype(jnp.bfloat16)
            for rows in (own_ref, other_ref)
        ],
        axis=0,
    )
    factor = math.log2(math.e) / math.sqrt(HEAD_SIZE)
    docs = row_docs[...]
    scores = []
    for i in range(5):
        product = lax.dot_general(
            queries, kv[i][:, :HEAD_SIZE], (((1,), (1,)), ((), ())), preferred_element_type=jnp.float32
        )
        allowed = docs == key_docs[:, i * PAIR : (i + 1) * PAIR]
        scores.append(jnp.where(allowed, product, NEG))
    highest = functools.reduce(jnp.maximum, [jnp.max(s, axis=1, keepdims=True) for s in scores])
    summed, mixed = 0.0, 0.0
    for i in range(5):
        part = jnp.exp2((scores[i] - highest) * factor)
        summed = summed + jnp.sum(part, axis=1, keepdims=True)
        mixed = mixed + jnp.dot(
            part.astype(jnp.bfloat16), kv[i][:, HEAD_SIZE:], preferred_element_type=jnp.float32
        )
    result = (mixed / summed).astype(jnp.bfloat16)
    columns = pl.ds(pl.multiple_of(slot * HEAD_SIZE, HEAD_SIZE), HEAD_SIZE)
    keep_ref[:, columns] = result[:ROWS]
    send_ref[:, columns] = result[ROWS:]


def one_head(shift, own, other, weight, kv, row_docs, key_docs, keep, send):
    inputs = [own, other, weight, *kv, row_docs, key_docs, keep, send]
    shape = jax.ShapeDtypeStruct(keep.shape, keep.dtype)
    return pl.pallas_call(
        functools.partial(head_kernel, shift),
        in_specs=[VMEM] * len(inputs),
        out_specs=[VMEM, VMEM],
        out_shape=[shape, shape],
        input_output_aliases={len(inputs) - 2: 0, len(inputs) - 1: 1},
        compiler_params=pltpu.CompilerParams(vmem_limit_bytes=12 * 2**20),
        cost_estimate=pl.CostEstimate(flops=2**28, bytes_accessed=2**21, transcendentals=2**18),
    )(*inputs)


def gate_kernel(*refs):
    pass


def gate(value, *after):
    return pl.pallas_call(
        gate_kernel,
        in_specs=[VMEM] * (1 + len(after)),
        out_specs=VMEM,
        out_shape=jax.ShapeDtypeStruct(value.shape, value.dtype),
        input_output_aliases={0: 0},
        compiler_params=pltpu.CompilerParams(vmem_limit_bytes=2**20),
    )(value, *after)


def join_kernel(mine_ref, other_ref, out_ref):
    y, x, z, c = place()
    out_ref[:, pl.ds(pl.multiple_of(c * HALF, HALF), HALF)] = mine_ref[...]
    out_ref[:, pl.ds(pl.multiple_of((1 - c) * HALF, HALF), HALF)] = other_ref[...]


def join(keep, arrived):
    return pl.pallas_call(
        join_kernel,
        grid=(1,),
        in_specs=[pl.BlockSpec((ROWS, HALF), lambda i: (0, 0))] * 2,
        out_specs=pl.BlockSpec((ROWS, 2 * HALF), lambda i: (0, 0)),
        out_shape=jax.ShapeDtypeStruct((ROWS, 2 * HALF), keep.dtype),
        compiler_params=pltpu.CompilerParams(vmem_limit_bytes=8 * 2**20),
    )(keep, arrived)


def body(tokens, query_weight, key_matrix, value_matrix, doc_lengths):
    other = swap_cores(tokens)
    weight = lax.ppermute(query_weight, AXES, first_moves())
    kv, row_docs, key_docs = kv_project(doc_lengths, tokens, other, key_matrix, value_matrix)
    kv_all = [kv] + [lax.ppermute(kv, AXES, moves(lambda c, d=d: (0, 0, d))) for d in AROUND[1:]]

    weight = gate(weight, *kv_all)
    arrivals = [(0, weight)]
    steps = (
        (4, lambda c: (1, 0, 1) if c == 0 else (-1, 0, -1)),
        (2, lambda c: (0, 1, 0)),
        (-2, lambda c: (0, -1, 0)),
        (3, lambda c: (1, 0, 0)),
        (-3, lambda c: (-1, 0, 0)),
        (1, lambda c: (0, 0, 1)),
        (-1, lambda c: (0, 0, -1)),
    )
    for shift, step in steps:
        arrivals.append((shift, lax.ppermute(weight, AXES, moves(step))))

    keep = jnp.zeros((ROWS, HALF), jnp.bfloat16)
    send = jnp.zeros((ROWS, HALF), jnp.bfloat16)
    for shift, w in arrivals:
        keep, send = one_head(shift, tokens, other, w, kv_all, row_docs, key_docs, keep, send)
    return join(keep, swap_cores(send))


def solution(mesh):
    in_specs = (P(("dp", "ctx"), None), P(None, "ctx"), P(), P(), P("dp"))
    out_specs = P(("dp", "ctx"), None)
    return jax.shard_map(body, mesh=mesh, in_specs=in_specs, out_specs=out_specs, check_vma=False)
```

```python
import functools
import math

import jax
import jax.numpy as jnp
from jax import lax
from jax.experimental import pallas as pl
from jax.experimental.pallas import tpu as pltpu
from jax.sharding import PartitionSpec as P

HEAD_SIZE = 128
WIDTH = 2048
ROWS = 128
PAIR = 2 * ROWS
HALF = 8 * HEAD_SIZE
NEG = -1e30

YS, XS, ZS, CORES = 8, 4, 8, 2
AXES = ("dp", "ctx")
ORDER = ((5, 3, 1, 7, 4, 2, 0, 6), (7, 3, 0, 6, 2, 4, 1, 5))
AROUND = (0, 1, -1, 2, -2)
VMEM = pl.BlockSpec(memory_space=pltpu.VMEM)
HBM = pl.BlockSpec(memory_space=pltpu.HBM)


def flat(y, x, z, c):
    return (((y % YS) * XS + x % XS) * ZS + z % ZS) * CORES + c


def everyone():
    return [(y, x, z, c) for y in range(YS) for x in range(XS) for z in range(ZS) for c in range(CORES)]


def first_moves():
    pairs = []
    for y, x, z, c in everyone():
        head = 8 * c + ORDER[c][(2 * x + 3 * y + z) % 8]
        pairs.append((flat(y, x, head // 2, head % 2), flat(y, x, z, c)))
    return pairs


def moves(step):
    pairs = []
    for y, x, z, c in everyone():
        dy, dx, dz = step(c)
        pairs.append((flat(y + dy, x + dx, z + dz, c), flat(y, x, z, c)))
    return pairs


def swap_cores(value):
    return lax.ppermute(value, AXES, [(flat(y, x, z, 1 - c), flat(y, x, z, c)) for y, x, z, c in everyone()])


def place():
    dp, ctx = lax.axis_index("dp"), lax.axis_index("ctx")
    return dp // XS, dp % XS, ctx // CORES, ctx % CORES


def kv_rows(rows, key_ref, value_ref, kv_ref, first):
    for base, matrix in ((0, key_ref), (PAIR, value_ref)):
        kv_ref[base + first : base + first + ROWS] = jnp.dot(
            rows[...], matrix[...], preferred_element_type=jnp.float32
        ).astype(jnp.bfloat16)


def own_kv_kernel(
    lengths_hbm, own_hbm, key_hbm, value_hbm, own_ref, key_ref, value_ref, kv_ref, row_docs_ref, key_docs_ref, lengths, sems
):
    y, x, z, c = place()
    mine = pl.ds(pl.multiple_of(c * HEAD_SIZE, HEAD_SIZE), HEAD_SIZE)
    copies = [
        pltpu.make_async_copy(own_hbm, own_ref, sems.at[0]),
        pltpu.make_async_copy(key_hbm.at[:, mine], key_ref, sems.at[1]),
        pltpu.make_async_copy(value_hbm.at[:, mine], value_ref, sems.at[2]),
        pltpu.make_async_copy(lengths_hbm, lengths, sems.at[3]),
    ]
    for copy in copies:
        copy.start()

    def positions(shape, axis, block):
        row = lax.broadcasted_iota(jnp.int32, shape, axis)
        return jnp.where(row < ROWS, row + ROWS * c, row - ROWS * c) + PAIR * block

    def docs(place_in_group):
        end = 0
        total = jnp.zeros(place_in_group.shape, jnp.int32)
        for e in range(16):
            end = end + lengths[e]
            total = total + (place_in_group >= end).astype(jnp.int32)
        return total

    copies[3].wait()
    row_docs_ref[...] = docs(positions((PAIR, 1), 0, z))
    for i, step in enumerate(AROUND):
        key_docs_ref[:, i * PAIR : (i + 1) * PAIR] = docs(positions((1, PAIR), 1, (z + step + ZS) % ZS))
    for copy in copies[:3]:
        copy.wait()
    kv_rows(own_ref, key_ref, value_ref, kv_ref, 0)


def own_kv(lengths, own, key_matrix, value_matrix):
    kind = jnp.bfloat16
    return pl.pallas_call(
        own_kv_kernel,
        in_specs=[HBM] * 4,
        out_specs=[VMEM] * 6,
        out_shape=[
            jax.ShapeDtypeStruct((ROWS, WIDTH), kind),
            jax.ShapeDtypeStruct((WIDTH, HEAD_SIZE), kind),
            jax.ShapeDtypeStruct((WIDTH, HEAD_SIZE), kind),
            jax.ShapeDtypeStruct((2 * PAIR, HEAD_SIZE), kind),
            jax.ShapeDtypeStruct((PAIR, 1), jnp.int32),
            jax.ShapeDtypeStruct((1, len(AROUND) * PAIR), jnp.int32),
        ],
        scratch_shapes=[pltpu.SMEM((16,), jnp.int32), pltpu.SemaphoreType.DMA((4,))],
        compiler_params=pltpu.CompilerParams(vmem_limit_bytes=52 * 2**20),
        cost_estimate=pl.CostEstimate(flops=2**27, bytes_accessed=2**21, transcendentals=0),
    )(lengths, own, key_matrix, value_matrix)


def other_kv_kernel(other_ref, key_ref, value_ref, held_ref, kv_ref):
    kv_rows(other_ref, key_ref, value_ref, kv_ref, ROWS)


def other_kv(other, key_mine, value_mine, kv):
    return pl.pallas_call(
        other_kv_kernel,
        in_specs=[VMEM] * 4,
        out_specs=VMEM,
        out_shape=jax.ShapeDtypeStruct(kv.shape, kv.dtype),
        input_output_aliases={3: 0},
        compiler_params=pltpu.CompilerParams(vmem_limit_bytes=8 * 2**20),
        cost_estimate=pl.CostEstimate(flops=2**27, bytes_accessed=2**21, transcendentals=0),
    )(other, key_mine, value_mine, kv)


def pack_kernel(weight_ref, kv_ref, first_ref, second_ref, same_ref, packed_ref):
    packed_ref[:WIDTH] = weight_ref[...]
    packed_ref[WIDTH:] = kv_ref[...]


def pack(weight, kv, after):
    rows = weight.shape[0] + kv.shape[0]
    return pl.pallas_call(
        pack_kernel,
        in_specs=[VMEM] * 4,
        out_specs=[VMEM] * 2,
        out_shape=[
            jax.ShapeDtypeStruct(weight.shape, weight.dtype),
            jax.ShapeDtypeStruct((rows, HEAD_SIZE), weight.dtype),
        ],
        input_output_aliases={0: 0},
        compiler_params=pltpu.CompilerParams(vmem_limit_bytes=4 * 2**20),
    )(weight, kv, *after)


def head_kernel(shift, bases, own_ref, other_ref, weight_ref, *refs):
    kv, (row_docs, key_docs, _, _, keep_ref, send_ref) = refs[:5], refs[5:]
    y, x, z, c = place()
    color = (2 * x + 3 * y + z + shift) % 8
    slot = 0
    for k in range(8):
        slot = slot + jnp.where(color == k, jnp.where(c == 0, ORDER[0][k], ORDER[1][k]), 0)
    queries = jnp.concatenate(
        [
            jnp.dot(rows[...], weight_ref[:WIDTH], preferred_element_type=jnp.float32).astype(jnp.bfloat16)
            for rows in (own_ref, other_ref)
        ],
        axis=0,
    )
    factor = math.log2(math.e) / math.sqrt(HEAD_SIZE)
    docs = row_docs[...]
    scores = []
    for i in range(5):
        product = lax.dot_general(
            queries, kv[i][bases[i] : bases[i] + PAIR], (((1,), (1,)), ((), ())), preferred_element_type=jnp.float32
        )
        allowed = docs == key_docs[:, i * PAIR : (i + 1) * PAIR]
        scores.append(jnp.where(allowed, product, NEG))
    highest = functools.reduce(jnp.maximum, [jnp.max(s, axis=1, keepdims=True) for s in scores])
    summed, mixed = 0.0, 0.0
    for i in range(5):
        part = jnp.exp2((scores[i] - highest) * factor)
        summed = summed + jnp.sum(part, axis=1, keepdims=True)
        mixed = mixed + jnp.dot(
            part.astype(jnp.bfloat16), kv[i][bases[i] + PAIR : bases[i] + 2 * PAIR], preferred_element_type=jnp.float32
        )
    result = (mixed / summed).astype(jnp.bfloat16)
    columns = pl.ds(pl.multiple_of(slot * HEAD_SIZE, HEAD_SIZE), HEAD_SIZE)
    keep_ref[:, columns] = result[:ROWS]
    send_ref[:, columns] = result[ROWS:]


def one_head(shift, own, other, weight, kv, row_docs, key_docs, keep, send):
    inputs = [own, other, weight, *kv, row_docs, key_docs, keep, send]
    bases = [array.shape[0] - 2 * PAIR for array in kv]
    shape = jax.ShapeDtypeStruct(keep.shape, keep.dtype)
    return pl.pallas_call(
        functools.partial(head_kernel, shift, bases),
        in_specs=[VMEM] * len(inputs),
        out_specs=[VMEM, VMEM],
        out_shape=[shape, shape],
        input_output_aliases={len(inputs) - 2: 0, len(inputs) - 1: 1},
        compiler_params=pltpu.CompilerParams(vmem_limit_bytes=12 * 2**20),
        cost_estimate=pl.CostEstimate(flops=2**28, bytes_accessed=2**21, transcendentals=2**18),
    )(*inputs)


def join_kernel(mine_ref, other_ref, out_ref):
    y, x, z, c = place()
    out_ref[:, pl.ds(pl.multiple_of(c * HALF, HALF), HALF)] = mine_ref[...]
    out_ref[:, pl.ds(pl.multiple_of((1 - c) * HALF, HALF), HALF)] = other_ref[...]


def join(keep, arrived):
    return pl.pallas_call(
        join_kernel,
        grid=(1,),
        in_specs=[pl.BlockSpec((ROWS, HALF), lambda i: (0, 0))] * 2,
        out_specs=pl.BlockSpec((ROWS, 2 * HALF), lambda i: (0, 0)),
        out_shape=jax.ShapeDtypeStruct((ROWS, 2 * HALF), keep.dtype),
        compiler_params=pltpu.CompilerParams(vmem_limit_bytes=8 * 2**20),
    )(keep, arrived)


def body(tokens, query_weight, key_matrix, value_matrix, doc_lengths):
    weight = lax.ppermute(query_weight, AXES, first_moves())
    own, key_mine, value_mine, kv, row_docs, key_docs = own_kv(doc_lengths, tokens, key_matrix, value_matrix)
    other = swap_cores(tokens)
    kv = other_kv(other, key_mine, value_mine, kv)
    far = [lax.ppermute(kv, AXES, moves(lambda c, d=d: (0, 0, d))) for d in (2, -2)]

    weight, packed = pack(weight, kv, far)
    above = lax.ppermute(packed, AXES, moves(lambda c: (0, 0, 1)))
    below = lax.ppermute(packed, AXES, moves(lambda c: (0, 0, -1)))
    arrivals = [(0, weight), (1, above), (-1, below)]
    steps = (
        (4, lambda c: (1, 0, 1) if c == 0 else (-1, 0, -1)),
        (2, lambda c: (0, 1, 0)),
        (-2, lambda c: (0, -1, 0)),
        (3, lambda c: (1, 0, 0)),
        (-3, lambda c: (-1, 0, 0)),
    )
    for shift, step in steps:
        arrivals.append((shift, lax.ppermute(weight, AXES, moves(step))))
    kv_all = [kv, above, below, *far]

    keep = jnp.zeros((ROWS, HALF), jnp.bfloat16)
    send = jnp.zeros((ROWS, HALF), jnp.bfloat16)
    for shift, w in arrivals:
        keep, send = one_head(shift, own, other, w, kv_all, row_docs, key_docs, keep, send)
    return join(keep, swap_cores(send))


def solution(mesh):
    in_specs = (P(("dp", "ctx"), None), P(None, "ctx"), P(), P(), P("dp"))
    out_specs = P(("dp", "ctx"), None)
    return jax.shard_map(body, mesh=mesh, in_specs=in_specs, out_specs=out_specs, check_vma=False)
```

```python
import functools
import math

import jax
import jax.numpy as jnp
from jax import lax
from jax.experimental import pallas as pl
from jax.experimental.pallas import tpu as pltpu
from jax.sharding import PartitionSpec as P

HEAD_SIZE = 128
WIDTH = 2048
ROWS = 128
PAIR = 2 * ROWS
HALF = 8 * HEAD_SIZE
NEG = -1e30

YS, XS, ZS, CORES = 8, 4, 8, 2
AXES = ("dp", "ctx")
ORDER = ((5, 3, 1, 7, 4, 2, 0, 6), (7, 3, 0, 6, 2, 4, 1, 5))
AROUND = (0, 1, -1, 2, -2)
VMEM = pl.BlockSpec(memory_space=pltpu.VMEM)
HBM = pl.BlockSpec(memory_space=pltpu.HBM)


def flat(y, x, z, c):
    return (((y % YS) * XS + x % XS) * ZS + z % ZS) * CORES + c


def everyone():
    return [(y, x, z, c) for y in range(YS) for x in range(XS) for z in range(ZS) for c in range(CORES)]


def first_moves():
    pairs = []
    for y, x, z, c in everyone():
        head = 8 * c + ORDER[c][(2 * x + 3 * y + z) % 8]
        pairs.append((flat(y, x, head // 2, head % 2), flat(y, x, z, c)))
    return pairs


def moves(step):
    pairs = []
    for y, x, z, c in everyone():
        dy, dx, dz = step(c)
        pairs.append((flat(y + dy, x + dx, z + dz, c), flat(y, x, z, c)))
    return pairs


def swap_cores(value):
    return lax.ppermute(value, AXES, [(flat(y, x, z, 1 - c), flat(y, x, z, c)) for y, x, z, c in everyone()])


def place():
    dp, ctx = lax.axis_index("dp"), lax.axis_index("ctx")
    return dp // XS, dp % XS, ctx // CORES, ctx % CORES


def kv_rows(rows, key_ref, value_ref, kv_ref, first):
    for base, matrix in ((0, key_ref), (PAIR, value_ref)):
        kv_ref[base + first : base + first + ROWS] = jnp.dot(
            rows[...], matrix[...], preferred_element_type=jnp.float32
        ).astype(jnp.bfloat16)


def own_kv_kernel(
    lengths_hbm, own_hbm, key_hbm, value_hbm, own_ref, key_ref, value_ref, kv_ref, row_docs_ref, key_docs_ref, lengths, sems
):
    y, x, z, c = place()
    mine = pl.ds(pl.multiple_of(c * HEAD_SIZE, HEAD_SIZE), HEAD_SIZE)
    copies = [
        pltpu.make_async_copy(own_hbm, own_ref, sems.at[0]),
        pltpu.make_async_copy(key_hbm.at[:, mine], key_ref, sems.at[1]),
        pltpu.make_async_copy(value_hbm.at[:, mine], value_ref, sems.at[2]),
        pltpu.make_async_copy(lengths_hbm, lengths, sems.at[3]),
    ]
    for copy in copies:
        copy.start()

    def positions(shape, axis, block):
        row = lax.broadcasted_iota(jnp.int32, shape, axis)
        return jnp.where(row < ROWS, row + ROWS * c, row - ROWS * c) + PAIR * block

    def docs(place_in_group):
        end = 0
        total = jnp.zeros(place_in_group.shape, jnp.int32)
        for e in range(16):
            end = end + lengths[e]
            total = total + (place_in_group >= end).astype(jnp.int32)
        return total

    copies[3].wait()
    row_docs_ref[...] = docs(positions((PAIR, 1), 0, z))
    for i, step in enumerate(AROUND):
        key_docs_ref[:, i * PAIR : (i + 1) * PAIR] = docs(positions((1, PAIR), 1, (z + step + ZS) % ZS))
    for copy in copies[:3]:
        copy.wait()
    kv_rows(own_ref, key_ref, value_ref, kv_ref, 0)


def own_kv(lengths, own, key_matrix, value_matrix):
    kind = jnp.bfloat16
    return pl.pallas_call(
        own_kv_kernel,
        in_specs=[HBM] * 4,
        out_specs=[VMEM] * 6,
        out_shape=[
            jax.ShapeDtypeStruct((ROWS, WIDTH), kind),
            jax.ShapeDtypeStruct((WIDTH, HEAD_SIZE), kind),
            jax.ShapeDtypeStruct((WIDTH, HEAD_SIZE), kind),
            jax.ShapeDtypeStruct((2 * PAIR, HEAD_SIZE), kind),
            jax.ShapeDtypeStruct((PAIR, 1), jnp.int32),
            jax.ShapeDtypeStruct((1, len(AROUND) * PAIR), jnp.int32),
        ],
        scratch_shapes=[pltpu.SMEM((16,), jnp.int32), pltpu.SemaphoreType.DMA((4,))],
        compiler_params=pltpu.CompilerParams(vmem_limit_bytes=52 * 2**20),
        cost_estimate=pl.CostEstimate(flops=2**27, bytes_accessed=2**21, transcendentals=0),
    )(lengths, own, key_matrix, value_matrix)


def other_kv_kernel(other_ref, key_ref, value_ref, held_ref, kv_ref):
    kv_rows(other_ref, key_ref, value_ref, kv_ref, ROWS)


def other_kv(other, key_mine, value_mine, kv):
    return pl.pallas_call(
        other_kv_kernel,
        in_specs=[VMEM] * 4,
        out_specs=VMEM,
        out_shape=jax.ShapeDtypeStruct(kv.shape, kv.dtype),
        input_output_aliases={3: 0},
        compiler_params=pltpu.CompilerParams(vmem_limit_bytes=8 * 2**20),
        cost_estimate=pl.CostEstimate(flops=2**27, bytes_accessed=2**21, transcendentals=0),
    )(other, key_mine, value_mine, kv)


def pack_kernel(weight_ref, above_ref, below_ref, same_ref, down_ref, up_ref):
    down_ref[:WIDTH] = weight_ref[...]
    down_ref[WIDTH:] = above_ref[...]
    up_ref[:WIDTH] = weight_ref[...]
    up_ref[WIDTH:] = below_ref[...]


def pack(weight, above, below):
    packed = jax.ShapeDtypeStruct((weight.shape[0] + above.shape[0], HEAD_SIZE), weight.dtype)
    return pl.pallas_call(
        pack_kernel,
        in_specs=[VMEM] * 3,
        out_specs=[VMEM] * 3,
        out_shape=[jax.ShapeDtypeStruct(weight.shape, weight.dtype), packed, packed],
        input_output_aliases={0: 0},
        compiler_params=pltpu.CompilerParams(vmem_limit_bytes=4 * 2**20),
    )(weight, above, below)


def choose_kernel(first_ref, second_ref, out_ref):
    y, x, z, c = place()

    @pl.when(c == 0)
    def _():
        out_ref[...] = first_ref[...]

    @pl.when(c == 1)
    def _():
        out_ref[...] = second_ref[...]


def choose(first, second):
    return pl.pallas_call(
        choose_kernel,
        in_specs=[VMEM] * 2,
        out_specs=VMEM,
        out_shape=jax.ShapeDtypeStruct(first.shape, first.dtype),
        compiler_params=pltpu.CompilerParams(vmem_limit_bytes=4 * 2**20),
    )(first, second)


def head_kernel(shift, bases, own_ref, other_ref, weight_ref, *refs):
    kv, (row_docs, key_docs, _, _, keep_ref, send_ref) = refs[:5], refs[5:]
    y, x, z, c = place()
    color = (2 * x + 3 * y + z + shift) % 8
    slot = 0
    for k in range(8):
        slot = slot + jnp.where(color == k, jnp.where(c == 0, ORDER[0][k], ORDER[1][k]), 0)
    queries = jnp.concatenate(
        [
            jnp.dot(rows[...], weight_ref[:WIDTH], preferred_element_type=jnp.float32).astype(jnp.bfloat16)
            for rows in (own_ref, other_ref)
        ],
        axis=0,
    )
    factor = math.log2(math.e) / math.sqrt(HEAD_SIZE)
    docs = row_docs[...]
    scores = []
    for i in range(5):
        product = lax.dot_general(
            queries, kv[i][bases[i] : bases[i] + PAIR], (((1,), (1,)), ((), ())), preferred_element_type=jnp.float32
        )
        allowed = docs == key_docs[:, i * PAIR : (i + 1) * PAIR]
        scores.append(jnp.where(allowed, product, NEG))
    highest = functools.reduce(jnp.maximum, [jnp.max(s, axis=1, keepdims=True) for s in scores])
    summed, mixed = 0.0, 0.0
    for i in range(5):
        part = jnp.exp2((scores[i] - highest) * factor)
        summed = summed + jnp.sum(part, axis=1, keepdims=True)
        mixed = mixed + jnp.dot(
            part.astype(jnp.bfloat16), kv[i][bases[i] + PAIR : bases[i] + 2 * PAIR], preferred_element_type=jnp.float32
        )
    result = (mixed / summed).astype(jnp.bfloat16)
    columns = pl.ds(pl.multiple_of(slot * HEAD_SIZE, HEAD_SIZE), HEAD_SIZE)
    keep_ref[:, columns] = result[:ROWS]
    send_ref[:, columns] = result[ROWS:]


def one_head(shift, own, other, weight, kv, row_docs, key_docs, keep, send):
    inputs = [own, other, weight, *kv, row_docs, key_docs, keep, send]
    bases = [array.shape[0] - 2 * PAIR for array in kv]
    shape = jax.ShapeDtypeStruct(keep.shape, keep.dtype)
    return pl.pallas_call(
        functools.partial(head_kernel, shift, bases),
        in_specs=[VMEM] * len(inputs),
        out_specs=[VMEM, VMEM],
        out_shape=[shape, shape],
        input_output_aliases={len(inputs) - 2: 0, len(inputs) - 1: 1},
        compiler_params=pltpu.CompilerParams(vmem_limit_bytes=12 * 2**20),
        cost_estimate=pl.CostEstimate(flops=2**28, bytes_accessed=2**21, transcendentals=2**18),
    )(*inputs)


def join_kernel(mine_ref, other_ref, out_ref):
    y, x, z, c = place()
    out_ref[:, pl.ds(pl.multiple_of(c * HALF, HALF), HALF)] = mine_ref[...]
    out_ref[:, pl.ds(pl.multiple_of((1 - c) * HALF, HALF), HALF)] = other_ref[...]


def join(keep, arrived):
    return pl.pallas_call(
        join_kernel,
        grid=(1,),
        in_specs=[pl.BlockSpec((ROWS, HALF), lambda i: (0, 0))] * 2,
        out_specs=pl.BlockSpec((ROWS, 2 * HALF), lambda i: (0, 0)),
        out_shape=jax.ShapeDtypeStruct((ROWS, 2 * HALF), keep.dtype),
        compiler_params=pltpu.CompilerParams(vmem_limit_bytes=8 * 2**20),
    )(keep, arrived)


def body(tokens, query_weight, key_matrix, value_matrix, doc_lengths):
    weight = lax.ppermute(query_weight, AXES, first_moves())
    own, key_mine, value_mine, kv, row_docs, key_docs = own_kv(doc_lengths, tokens, key_matrix, value_matrix)
    other = swap_cores(tokens)
    kv = other_kv(other, key_mine, value_mine, kv)
    near = [lax.ppermute(kv, AXES, moves(lambda c, d=d: (0, 0, d))) for d in (1, -1)]

    weight, down, up = pack(weight, *near)
    right = lax.ppermute(weight, AXES, moves(lambda c: (0, 1, 0)))
    left = lax.ppermute(weight, AXES, moves(lambda c: (0, -1, 0)))
    above = lax.ppermute(down, AXES, moves(lambda c: (0, 0, 1)))
    below = lax.ppermute(up, AXES, moves(lambda c: (0, 0, -1)))
    front = lax.ppermute(weight, AXES, moves(lambda c: (1, 0, 0)))
    back = lax.ppermute(weight, AXES, moves(lambda c: (-1, 0, 0)))
    across = lax.ppermute(choose(right, left), AXES, moves(lambda c: (0, 1, 0) if c == 0 else (0, -1, 0)))
    arrivals = [(0, weight), (2, right), (-2, left), (1, above), (-1, below), (3, front), (-3, back), (4, across)]
    kv_all = [kv, *near, above, below]

    keep = jnp.zeros((ROWS, HALF), jnp.bfloat16)
    send = jnp.zeros((ROWS, HALF), jnp.bfloat16)
    for shift, w in arrivals:
        keep, send = one_head(shift, own, other, w, kv_all, row_docs, key_docs, keep, send)
    return join(keep, swap_cores(send))


def solution(mesh):
    in_specs = (P(("dp", "ctx"), None), P(None, "ctx"), P(), P(), P("dp"))
    out_specs = P(("dp", "ctx"), None)
    return jax.shard_map(body, mesh=mesh, in_specs=in_specs, out_specs=out_specs, check_vma=False)
```

```python
import functools
import math

import jax
import jax.numpy as jnp
from jax import lax
from jax.experimental import pallas as pl
from jax.experimental.pallas import tpu as pltpu
from jax.sharding import PartitionSpec as P

HEAD_SIZE = 128
WIDTH = 2048
ROWS = 128
PAIR = 2 * ROWS
HALF = 8 * HEAD_SIZE
NEG = -1e30

YS, XS, ZS, CORES = 8, 4, 8, 2
AXES = ("dp", "ctx")
ORDER = ((5, 3, 1, 7, 4, 2, 0, 6), (7, 3, 0, 6, 2, 4, 1, 5))
AROUND = (0, 1, -1, 2, -2)
VMEM = pl.BlockSpec(memory_space=pltpu.VMEM)
HBM = pl.BlockSpec(memory_space=pltpu.HBM)


def flat(y, x, z, c):
    return (((y % YS) * XS + x % XS) * ZS + z % ZS) * CORES + c


def everyone():
    return [(y, x, z, c) for y in range(YS) for x in range(XS) for z in range(ZS) for c in range(CORES)]


def first_moves():
    pairs = []
    for y, x, z, c in everyone():
        head = 8 * c + ORDER[c][(2 * x + 3 * y + z) % 8]
        pairs.append((flat(y, x, head // 2, head % 2), flat(y, x, z, c)))
    return pairs


def moves(step):
    pairs = []
    for y, x, z, c in everyone():
        dy, dx, dz = step(c)
        pairs.append((flat(y + dy, x + dx, z + dz, c), flat(y, x, z, c)))
    return pairs


def swap_cores(value):
    return lax.ppermute(value, AXES, [(flat(y, x, z, 1 - c), flat(y, x, z, c)) for y, x, z, c in everyone()])


def place():
    dp, ctx = lax.axis_index("dp"), lax.axis_index("ctx")
    return dp // XS, dp % XS, ctx // CORES, ctx % CORES


def kv_rows(rows, key_ref, value_ref, kv_ref, first):
    for base, matrix in ((0, key_ref), (PAIR, value_ref)):
        kv_ref[base + first : base + first + ROWS] = jnp.dot(
            rows[...], matrix[...], preferred_element_type=jnp.float32
        ).astype(jnp.bfloat16)


def own_kv_kernel(
    lengths_hbm, own_hbm, key_hbm, value_hbm, own_ref, key_ref, value_ref, kv_ref, row_docs_ref, key_docs_ref, lengths, sems
):
    y, x, z, c = place()
    mine = pl.ds(pl.multiple_of(c * HEAD_SIZE, HEAD_SIZE), HEAD_SIZE)
    copies = [
        pltpu.make_async_copy(own_hbm, own_ref, sems.at[0]),
        pltpu.make_async_copy(key_hbm.at[:, mine], key_ref, sems.at[1]),
        pltpu.make_async_copy(value_hbm.at[:, mine], value_ref, sems.at[2]),
        pltpu.make_async_copy(lengths_hbm, lengths, sems.at[3]),
    ]
    for copy in copies:
        copy.start()

    def positions(shape, axis, block):
        row = lax.broadcasted_iota(jnp.int32, shape, axis)
        return jnp.where(row < ROWS, row + ROWS * c, row - ROWS * c) + PAIR * block

    def docs(place_in_group):
        end = 0
        total = jnp.zeros(place_in_group.shape, jnp.int32)
        for e in range(16):
            end = end + lengths[e]
            total = total + (place_in_group >= end).astype(jnp.int32)
        return total

    copies[3].wait()
    row_docs_ref[...] = docs(positions((PAIR, 1), 0, z))
    for i, step in enumerate(AROUND):
        key_docs_ref[:, i * PAIR : (i + 1) * PAIR] = docs(positions((1, PAIR), 1, (z + step + ZS) % ZS))
    for copy in copies[:3]:
        copy.wait()
    kv_rows(own_ref, key_ref, value_ref, kv_ref, 0)


def own_kv(lengths, own, key_matrix, value_matrix):
    kind = jnp.bfloat16
    return pl.pallas_call(
        own_kv_kernel,
        in_specs=[HBM] * 4,
        out_specs=[VMEM] * 6,
        out_shape=[
            jax.ShapeDtypeStruct((ROWS, WIDTH), kind),
            jax.ShapeDtypeStruct((WIDTH, HEAD_SIZE), kind),
            jax.ShapeDtypeStruct((WIDTH, HEAD_SIZE), kind),
            jax.ShapeDtypeStruct((2 * PAIR, HEAD_SIZE), kind),
            jax.ShapeDtypeStruct((PAIR, 1), jnp.int32),
            jax.ShapeDtypeStruct((1, len(AROUND) * PAIR), jnp.int32),
        ],
        scratch_shapes=[pltpu.SMEM((16,), jnp.int32), pltpu.SemaphoreType.DMA((4,))],
        compiler_params=pltpu.CompilerParams(vmem_limit_bytes=52 * 2**20),
        cost_estimate=pl.CostEstimate(flops=2**27, bytes_accessed=2**21, transcendentals=0),
    )(lengths, own, key_matrix, value_matrix)


def other_kv_kernel(other_ref, key_ref, value_ref, held_ref, kv_ref):
    kv_rows(other_ref, key_ref, value_ref, kv_ref, ROWS)


def other_kv(other, key_mine, value_mine, kv):
    return pl.pallas_call(
        other_kv_kernel,
        in_specs=[VMEM] * 4,
        out_specs=VMEM,
        out_shape=jax.ShapeDtypeStruct(kv.shape, kv.dtype),
        input_output_aliases={3: 0},
        compiler_params=pltpu.CompilerParams(vmem_limit_bytes=8 * 2**20),
        cost_estimate=pl.CostEstimate(flops=2**27, bytes_accessed=2**21, transcendentals=0),
    )(other, key_mine, value_mine, kv)


def gate_kernel(*refs):
    pass


def gate(value, *after):
    return pl.pallas_call(
        gate_kernel,
        in_specs=[VMEM] * (1 + len(after)),
        out_specs=VMEM,
        out_shape=jax.ShapeDtypeStruct(value.shape, value.dtype),
        input_output_aliases={0: 0},
        compiler_params=pltpu.CompilerParams(vmem_limit_bytes=2**20),
    )(value, *after)


def pack_kernel(weight_ref, above_ref, below_ref, down_ref, up_ref):
    down_ref[:WIDTH] = weight_ref[...]
    down_ref[WIDTH:] = above_ref[...]
    up_ref[:WIDTH] = weight_ref[...]
    up_ref[WIDTH:] = below_ref[...]


def pack(weight, above, below):
    packed = jax.ShapeDtypeStruct((weight.shape[0] + above.shape[0], HEAD_SIZE), weight.dtype)
    return pl.pallas_call(
        pack_kernel,
        in_specs=[VMEM] * 3,
        out_specs=[VMEM] * 2,
        out_shape=[packed, packed],
        compiler_params=pltpu.CompilerParams(vmem_limit_bytes=4 * 2**20),
    )(weight, above, below)


def choose_kernel(first_ref, second_ref, out_ref):
    y, x, z, c = place()

    @pl.when(c == 0)
    def _():
        out_ref[...] = first_ref[...]

    @pl.when(c == 1)
    def _():
        out_ref[...] = second_ref[...]


def choose(first, second):
    return pl.pallas_call(
        choose_kernel,
        in_specs=[VMEM] * 2,
        out_specs=VMEM,
        out_shape=jax.ShapeDtypeStruct(first.shape, first.dtype),
        compiler_params=pltpu.CompilerParams(vmem_limit_bytes=4 * 2**20),
    )(first, second)


def attend(queries, kv, bases, docs, key_docs):
    factor = math.log2(math.e) / math.sqrt(HEAD_SIZE)
    scores = []
    for i in range(5):
        product = lax.dot_general(
            queries, kv[i][bases[i] : bases[i] + PAIR], (((1,), (1,)), ((), ())), preferred_element_type=jnp.float32
        )
        allowed = docs == key_docs[:, i * PAIR : (i + 1) * PAIR]
        scores.append(jnp.where(allowed, product, NEG))
    highest = functools.reduce(jnp.maximum, [jnp.max(s, axis=1, keepdims=True) for s in scores])
    summed, mixed = 0.0, 0.0
    for i in range(5):
        part = jnp.exp2((scores[i] - highest) * factor)
        summed = summed + jnp.sum(part, axis=1, keepdims=True)
        mixed = mixed + jnp.dot(
            part.astype(jnp.bfloat16), kv[i][bases[i] + PAIR : bases[i] + 2 * PAIR], preferred_element_type=jnp.float32
        )
    return (mixed / summed).astype(jnp.bfloat16)


def heads_kernel(shifts, bases, own_ref, other_ref, *refs):
    weights, refs = refs[: len(shifts)], refs[len(shifts) :]
    kv, (row_docs, key_docs, _, _, keep_ref, send_ref) = refs[:5], refs[5:]
    y, x, z, c = place()
    docs = row_docs[...]
    for first in range(0, len(shifts), 2):
        pair = weights[first : first + 2]
        matrix = jnp.concatenate([w[:WIDTH] for w in pair], axis=1)
        queries = jnp.concatenate(
            [
                jnp.dot(rows[...], matrix, preferred_element_type=jnp.float32).astype(jnp.bfloat16)
                for rows in (own_ref, other_ref)
            ],
            axis=0,
        )
        for i, shift in enumerate(shifts[first : first + 2]):
            color = (2 * x + 3 * y + z + shift) % 8
            slot = 0
            for k in range(8):
                slot = slot + jnp.where(color == k, jnp.where(c == 0, ORDER[0][k], ORDER[1][k]), 0)
            result = attend(queries[:, i * HEAD_SIZE : (i + 1) * HEAD_SIZE], kv, bases, docs, key_docs)
            columns = pl.ds(pl.multiple_of(slot * HEAD_SIZE, HEAD_SIZE), HEAD_SIZE)
            keep_ref[:, columns] = result[:ROWS]
            send_ref[:, columns] = result[ROWS:]


def some_heads(arrivals, own, other, kv, row_docs, key_docs, keep, send):
    inputs = [own, other, *(w for _, w in arrivals), *kv, row_docs, key_docs, keep, send]
    bases = [array.shape[0] - 2 * PAIR for array in kv]
    shape = jax.ShapeDtypeStruct(keep.shape, keep.dtype)
    return pl.pallas_call(
        functools.partial(heads_kernel, tuple(shift for shift, _ in arrivals), bases),
        in_specs=[VMEM] * len(inputs),
        out_specs=[VMEM, VMEM],
        out_shape=[shape, shape],
        input_output_aliases={len(inputs) - 2: 0, len(inputs) - 1: 1},
        compiler_params=pltpu.CompilerParams(vmem_limit_bytes=16 * 2**20),
        cost_estimate=pl.CostEstimate(flops=2**28, bytes_accessed=2**21, transcendentals=2**18),
    )(*inputs)


def join_kernel(mine_ref, other_ref, out_ref):
    y, x, z, c = place()
    out_ref[:, pl.ds(pl.multiple_of(c * HALF, HALF), HALF)] = mine_ref[...]
    out_ref[:, pl.ds(pl.multiple_of((1 - c) * HALF, HALF), HALF)] = other_ref[...]


def join(keep, arrived):
    return pl.pallas_call(
        join_kernel,
        grid=(1,),
        in_specs=[pl.BlockSpec((ROWS, HALF), lambda i: (0, 0))] * 2,
        out_specs=pl.BlockSpec((ROWS, 2 * HALF), lambda i: (0, 0)),
        out_shape=jax.ShapeDtypeStruct((ROWS, 2 * HALF), keep.dtype),
        compiler_params=pltpu.CompilerParams(vmem_limit_bytes=8 * 2**20),
    )(keep, arrived)


def body(tokens, query_weight, key_matrix, value_matrix, doc_lengths):
    weight = lax.ppermute(query_weight, AXES, first_moves())
    own, key_mine, value_mine, kv, row_docs, key_docs = own_kv(doc_lengths, tokens, key_matrix, value_matrix)
    other = swap_cores(tokens)
    kv = other_kv(other, key_mine, value_mine, kv)
    near = [lax.ppermute(kv, AXES, moves(lambda c, d=d: (0, 0, d))) for d in (1, -1)]

    weight = gate(weight, *near)
    right = lax.ppermute(weight, AXES, moves(lambda c: (0, 1, 0)))
    left = lax.ppermute(weight, AXES, moves(lambda c: (0, -1, 0)))
    down, up = pack(weight, *near)
    above = lax.ppermute(down, AXES, moves(lambda c: (0, 0, 1)))
    below = lax.ppermute(up, AXES, moves(lambda c: (0, 0, -1)))
    front = lax.ppermute(weight, AXES, moves(lambda c: (1, 0, 0)))
    back = lax.ppermute(weight, AXES, moves(lambda c: (-1, 0, 0)))
    across = lax.ppermute(choose(right, left), AXES, moves(lambda c: (0, 1, 0) if c == 0 else (0, -1, 0)))
    arrivals = [(0, weight), (2, right), (-2, left), (1, above), (-1, below), (3, front), (-3, back), (4, across)]
    kv_all = [kv, *near, above, below]

    keep = jnp.zeros((ROWS, HALF), jnp.bfloat16)
    send = jnp.zeros((ROWS, HALF), jnp.bfloat16)
    for some in (arrivals[:4], arrivals[4:6], arrivals[6:]):
        keep, send = some_heads(some, own, other, kv_all, row_docs, key_docs, keep, send)
    return join(keep, swap_cores(send))


def solution(mesh):
    in_specs = (P(("dp", "ctx"), None), P(None, "ctx"), P(), P(), P("dp"))
    out_specs = P(("dp", "ctx"), None)
    return jax.shard_map(body, mesh=mesh, in_specs=in_specs, out_specs=out_specs, check_vma=False)
```

```python
import functools
import math

import jax
import jax.numpy as jnp
from jax import lax
from jax.experimental import pallas as pl
from jax.experimental.pallas import tpu as pltpu
from jax.sharding import PartitionSpec as P

HEAD_SIZE = 128
WIDTH = 2048
ROWS = 128
PAIR = 2 * ROWS
HALF = 8 * HEAD_SIZE
NEG = -1e30

YS, XS, ZS, CORES = 8, 4, 8, 2
AXES = ("dp", "ctx")
KV_ROWS = 2 * PAIR
AROUND = (0, 1, -1, 2, -2)
VMEM = pl.BlockSpec(memory_space=pltpu.VMEM)
HBM = pl.BlockSpec(memory_space=pltpu.HBM)


def flat(y, x, z, c):
    return (((y % YS) * XS + x % XS) * ZS + z % ZS) * CORES + c


def everyone():
    return [(y, x, z, c) for y in range(YS) for x in range(XS) for z in range(ZS) for c in range(CORES)]


def color_of(y, x, z):
    return (2 * x + y + 3 * z) % 8


def first_moves():
    pairs = []
    for y, x, z, c in everyone():
        pairs.append((flat(y, x, color_of(y, x, z), c), flat(y, x, z, c)))
    return pairs


def moves(step):
    pairs = []
    for y, x, z, c in everyone():
        dy, dx, dz = step(c)
        pairs.append((flat(y + dy, x + dx, z + dz, c), flat(y, x, z, c)))
    return pairs


def swap_cores(value):
    return lax.ppermute(value, AXES, [(flat(y, x, z, 1 - c), flat(y, x, z, c)) for y, x, z, c in everyone()])


def place():
    dp, ctx = lax.axis_index("dp"), lax.axis_index("ctx")
    return dp // XS, dp % XS, ctx // CORES, ctx % CORES


def kv_rows(rows, key_ref, value_ref, kv_ref, first):
    for base, matrix in ((0, key_ref), (PAIR, value_ref)):
        product = jnp.dot(rows[...], matrix[...], preferred_element_type=jnp.float32).astype(jnp.bfloat16)
        for j in range(2):
            start = j * KV_ROWS + base + first
            kv_ref[start : start + ROWS] = product[:, j * HEAD_SIZE : (j + 1) * HEAD_SIZE]


def own_kv_kernel(
    lengths_hbm, own_hbm, key_hbm, value_hbm, own_ref, key_ref, value_ref, kv_ref, row_docs_ref, key_docs_ref, lengths, sems
):
    y, x, z, c = place()
    copies = [
        pltpu.make_async_copy(own_hbm, own_ref, sems.at[0]),
        pltpu.make_async_copy(key_hbm, key_ref, sems.at[1]),
        pltpu.make_async_copy(value_hbm, value_ref, sems.at[2]),
        pltpu.make_async_copy(lengths_hbm, lengths, sems.at[3]),
    ]
    for copy in copies:
        copy.start()

    def positions(shape, axis, block):
        row = lax.broadcasted_iota(jnp.int32, shape, axis)
        return jnp.where(row < ROWS, row + ROWS * c, row - ROWS * c) + PAIR * block

    def docs(place_in_group):
        end = 0
        total = jnp.zeros(place_in_group.shape, jnp.int32)
        for e in range(16):
            end = end + lengths[e]
            total = total + (place_in_group >= end).astype(jnp.int32)
        return total

    copies[3].wait()
    row_docs_ref[...] = docs(positions((PAIR, 1), 0, z))
    for i, step in enumerate(AROUND):
        key_docs_ref[:, i * PAIR : (i + 1) * PAIR] = docs(positions((1, PAIR), 1, (z + step + ZS) % ZS))
    for copy in copies[:3]:
        copy.wait()
    kv_rows(own_ref, key_ref, value_ref, kv_ref, 0)


def own_kv(lengths, own, key_matrix, value_matrix):
    kind = jnp.bfloat16
    return pl.pallas_call(
        own_kv_kernel,
        in_specs=[HBM] * 4,
        out_specs=[VMEM] * 6,
        out_shape=[
            jax.ShapeDtypeStruct((ROWS, WIDTH), kind),
            jax.ShapeDtypeStruct((WIDTH, 2 * HEAD_SIZE), kind),
            jax.ShapeDtypeStruct((WIDTH, 2 * HEAD_SIZE), kind),
            jax.ShapeDtypeStruct((2 * KV_ROWS, HEAD_SIZE), kind),
            jax.ShapeDtypeStruct((PAIR, 1), jnp.int32),
            jax.ShapeDtypeStruct((1, len(AROUND) * PAIR), jnp.int32),
        ],
        scratch_shapes=[pltpu.SMEM((16,), jnp.int32), pltpu.SemaphoreType.DMA((4,))],
        compiler_params=pltpu.CompilerParams(vmem_limit_bytes=50 * 2**20),
        cost_estimate=pl.CostEstimate(flops=2**27, bytes_accessed=2**21, transcendentals=0),
    )(lengths, own, key_matrix, value_matrix)


def other_kv_kernel(other_ref, key_ref, value_ref, held_ref, kv_ref):
    kv_rows(other_ref, key_ref, value_ref, kv_ref, ROWS)


def other_kv(other, key_mine, value_mine, kv):
    return pl.pallas_call(
        other_kv_kernel,
        in_specs=[VMEM] * 4,
        out_specs=VMEM,
        out_shape=jax.ShapeDtypeStruct(kv.shape, kv.dtype),
        input_output_aliases={3: 0},
        compiler_params=pltpu.CompilerParams(vmem_limit_bytes=8 * 2**20),
        cost_estimate=pl.CostEstimate(flops=2**27, bytes_accessed=2**21, transcendentals=0),
    )(other, key_mine, value_mine, kv)


def gate_kernel(*refs):
    pass


def gate(value, *after):
    return pl.pallas_call(
        gate_kernel,
        in_specs=[VMEM] * (1 + len(after)),
        out_specs=VMEM,
        out_shape=jax.ShapeDtypeStruct(value.shape, value.dtype),
        input_output_aliases={0: 0},
        compiler_params=pltpu.CompilerParams(vmem_limit_bytes=2**20),
    )(value, *after)


def pack_kernel(weight_ref, above_ref, below_ref, down_ref, up_ref):
    down_ref[:WIDTH] = weight_ref[...]
    down_ref[WIDTH:] = above_ref[...]
    up_ref[:WIDTH] = weight_ref[...]
    up_ref[WIDTH:] = below_ref[...]


def pack(weight, above, below):
    packed = jax.ShapeDtypeStruct((weight.shape[0] + above.shape[0], HEAD_SIZE), weight.dtype)
    return pl.pallas_call(
        pack_kernel,
        in_specs=[VMEM] * 3,
        out_specs=[VMEM] * 2,
        out_shape=[packed, packed],
        compiler_params=pltpu.CompilerParams(vmem_limit_bytes=4 * 2**20),
    )(weight, above, below)


def choose_kernel(first_ref, second_ref, out_ref):
    y, x, z, c = place()

    @pl.when(c == 0)
    def _():
        out_ref[...] = first_ref[...]

    @pl.when(c == 1)
    def _():
        out_ref[...] = second_ref[...]


def choose(first, second):
    return pl.pallas_call(
        choose_kernel,
        in_specs=[VMEM] * 2,
        out_specs=VMEM,
        out_shape=jax.ShapeDtypeStruct(first.shape, first.dtype),
        compiler_params=pltpu.CompilerParams(vmem_limit_bytes=4 * 2**20),
    )(first, second)


def attend(queries, kv, bases, half, docs, key_docs):
    def rows(i, more):
        start = pl.multiple_of(bases[i] + more + half * KV_ROWS, PAIR)
        return kv[i][pl.ds(start, PAIR)]

    factor = math.log2(math.e) / math.sqrt(HEAD_SIZE)
    scores = []
    for i in range(5):
        product = lax.dot_general(
            queries, rows(i, 0), (((1,), (1,)), ((), ())), preferred_element_type=jnp.float32
        )
        allowed = docs == key_docs[:, i * PAIR : (i + 1) * PAIR]
        scores.append(jnp.where(allowed, product, NEG))
    highest = functools.reduce(jnp.maximum, [jnp.max(s, axis=1, keepdims=True) for s in scores])
    summed, mixed = 0.0, 0.0
    for i in range(5):
        part = jnp.exp2((scores[i] - highest) * factor)
        summed = summed + jnp.sum(part, axis=1, keepdims=True)
        mixed = mixed + jnp.dot(
            part.astype(jnp.bfloat16), rows(i, PAIR), preferred_element_type=jnp.float32
        )
    return (mixed / summed).astype(jnp.bfloat16)


def heads_kernel(shifts, bases, own_ref, other_ref, *refs):
    weights, refs = refs[: len(shifts)], refs[len(shifts) :]
    kv, (row_docs, key_docs, _, _, keep_ref, send_ref) = refs[:5], refs[5:]
    y, x, z, c = place()
    docs = row_docs[...]
    for first in range(0, len(shifts), 2):
        pair = weights[first : first + 2]
        matrix = jnp.concatenate([w[:WIDTH] for w in pair], axis=1)
        queries = jnp.concatenate(
            [
                jnp.dot(rows[...], matrix, preferred_element_type=jnp.float32).astype(jnp.bfloat16)
                for rows in (own_ref, other_ref)
            ],
            axis=0,
        )
        for i, shift in enumerate(shifts[first : first + 2]):
            color = (color_of(y, x, z) + shift + 8) % 8
            result = attend(queries[:, i * HEAD_SIZE : (i + 1) * HEAD_SIZE], kv, bases, color // 4, docs, key_docs)
            columns = pl.ds(pl.multiple_of(color * HEAD_SIZE, HEAD_SIZE), HEAD_SIZE)
            keep_ref[:, columns] = result[:ROWS]
            send_ref[:, columns] = result[ROWS:]


def some_heads(arrivals, own, other, kv, row_docs, key_docs, keep, send):
    inputs = [own, other, *(w for _, w in arrivals), *kv, row_docs, key_docs, keep, send]
    bases = [array.shape[0] - 2 * KV_ROWS for array in kv]
    shape = jax.ShapeDtypeStruct(keep.shape, keep.dtype)
    return pl.pallas_call(
        functools.partial(heads_kernel, tuple(shift for shift, _ in arrivals), bases),
        in_specs=[VMEM] * len(inputs),
        out_specs=[VMEM, VMEM],
        out_shape=[shape, shape],
        input_output_aliases={len(inputs) - 2: 0, len(inputs) - 1: 1},
        compiler_params=pltpu.CompilerParams(vmem_limit_bytes=16 * 2**20),
        cost_estimate=pl.CostEstimate(flops=2**28, bytes_accessed=2**21, transcendentals=2**18),
    )(*inputs)


def join_kernel(mine_ref, other_ref, out_ref):
    y, x, z, c = place()
    for k in range(8):
        columns = slice(k * HEAD_SIZE, (k + 1) * HEAD_SIZE)
        for core, ref in ((c, mine_ref), (1 - c, other_ref)):
            start = pl.multiple_of((2 * k + core) * HEAD_SIZE, HEAD_SIZE)
            out_ref[:, pl.ds(start, HEAD_SIZE)] = ref[:, columns]


def join(keep, arrived):
    return pl.pallas_call(
        join_kernel,
        grid=(1,),
        in_specs=[pl.BlockSpec((ROWS, HALF), lambda i: (0, 0))] * 2,
        out_specs=pl.BlockSpec((ROWS, 2 * HALF), lambda i: (0, 0)),
        out_shape=jax.ShapeDtypeStruct((ROWS, 2 * HALF), keep.dtype),
        compiler_params=pltpu.CompilerParams(vmem_limit_bytes=8 * 2**20),
    )(keep, arrived)


def body(tokens, query_weight, key_matrix, value_matrix, doc_lengths):
    weight = lax.ppermute(query_weight, AXES, first_moves())
    own, key_mine, value_mine, kv, row_docs, key_docs = own_kv(doc_lengths, tokens, key_matrix, value_matrix)
    other = swap_cores(tokens)
    kv = other_kv(other, key_mine, value_mine, kv)
    near = [lax.ppermute(kv, AXES, moves(lambda c, d=d: (0, 0, d))) for d in (1, -1)]

    weight = gate(weight, *near)
    right = lax.ppermute(weight, AXES, moves(lambda c: (0, 1, 0)))
    left = lax.ppermute(weight, AXES, moves(lambda c: (0, -1, 0)))
    down, up = pack(weight, *near)
    above = lax.ppermute(down, AXES, moves(lambda c: (0, 0, 1)))
    below = lax.ppermute(up, AXES, moves(lambda c: (0, 0, -1)))
    front = lax.ppermute(weight, AXES, moves(lambda c: (1, 0, 0)))
    back = lax.ppermute(weight, AXES, moves(lambda c: (-1, 0, 0)))
    across = lax.ppermute(choose(right, left), AXES, moves(lambda c: (0, 1, 0) if c == 0 else (0, -1, 0)))
    arrivals = [(0, weight), (2, right), (-2, left), (3, above), (-3, below), (1, front), (-1, back), (4, across)]
    kv_all = [kv, *near, above, below]

    keep = jnp.zeros((ROWS, HALF), jnp.bfloat16)
    send = jnp.zeros((ROWS, HALF), jnp.bfloat16)
    for some in (arrivals[:4], arrivals[4:6], arrivals[6:]):
        keep, send = some_heads(some, own, other, kv_all, row_docs, key_docs, keep, send)
    return join(keep, swap_cores(send))


def solution(mesh):
    in_specs = (P(("dp", "ctx"), None), P(None, "ctx"), P(), P(), P("dp"))
    out_specs = P(("dp", "ctx"), None)
    return jax.shard_map(body, mesh=mesh, in_specs=in_specs, out_specs=out_specs, check_vma=False)
```

```python
import functools
import math

import jax
import jax.numpy as jnp
from jax import lax
from jax.experimental import pallas as pl
from jax.experimental.pallas import tpu as pltpu
from jax.sharding import PartitionSpec as P

HEAD_SIZE = 128
WIDTH = 2048
ROWS = 128
PAIR = 2 * ROWS
HALF = 8 * HEAD_SIZE
NEG = -1e30

YS, XS, ZS, CORES = 8, 4, 8, 2
AXES = ("dp", "ctx")
ORDER = ((5, 3, 1, 7, 4, 2, 0, 6), (7, 3, 0, 6, 2, 4, 1, 5))
AROUND = (0, 1, -1, 2, -2)
VMEM = pl.BlockSpec(memory_space=pltpu.VMEM)
HBM = pl.BlockSpec(memory_space=pltpu.HBM)


def flat(y, x, z, c):
    return (((y % YS) * XS + x % XS) * ZS + z % ZS) * CORES + c


def everyone():
    return [(y, x, z, c) for y in range(YS) for x in range(XS) for z in range(ZS) for c in range(CORES)]


def first_moves():
    pairs = []
    for y, x, z, c in everyone():
        head = 8 * c + ORDER[c][(2 * x + 3 * y + z) % 8]
        pairs.append((flat(y, x, head // 2, head % 2), flat(y, x, z, c)))
    return pairs


def moves(step):
    pairs = []
    for y, x, z, c in everyone():
        dy, dx, dz = step(c)
        pairs.append((flat(y + dy, x + dx, z + dz, c), flat(y, x, z, c)))
    return pairs


def swap_cores(value):
    return lax.ppermute(value, AXES, [(flat(y, x, z, 1 - c), flat(y, x, z, c)) for y, x, z, c in everyone()])


def place():
    dp, ctx = lax.axis_index("dp"), lax.axis_index("ctx")
    return dp // XS, dp % XS, ctx // CORES, ctx % CORES


def kv_rows(rows, key_ref, value_ref, kv_ref, first):
    for base, matrix in ((0, key_ref), (PAIR, value_ref)):
        kv_ref[base + first : base + first + ROWS] = jnp.dot(
            rows[...], matrix[...], preferred_element_type=jnp.float32
        ).astype(jnp.bfloat16)


def own_kv_kernel(
    lengths_hbm, own_hbm, key_hbm, value_hbm, own_ref, key_ref, value_ref, kv_ref, row_docs_ref, key_docs_ref, lengths, sems
):
    y, x, z, c = place()
    mine = pl.ds(pl.multiple_of(c * HEAD_SIZE, HEAD_SIZE), HEAD_SIZE)
    copies = [
        pltpu.make_async_copy(own_hbm, own_ref, sems.at[0]),
        pltpu.make_async_copy(key_hbm.at[:, mine], key_ref, sems.at[1]),
        pltpu.make_async_copy(value_hbm.at[:, mine], value_ref, sems.at[2]),
        pltpu.make_async_copy(lengths_hbm, lengths, sems.at[3]),
    ]
    for copy in copies:
        copy.start()

    def positions(shape, axis, block):
        row = lax.broadcasted_iota(jnp.int32, shape, axis)
        return jnp.where(row < ROWS, row + ROWS * c, row - ROWS * c) + PAIR * block

    def docs(place_in_group):
        end = 0
        total = jnp.zeros(place_in_group.shape, jnp.int32)
        for e in range(16):
            end = end + lengths[e]
            total = total + (place_in_group >= end).astype(jnp.int32)
        return total

    copies[3].wait()
    row_docs_ref[...] = docs(positions((PAIR, 1), 0, z))
    for i, step in enumerate(AROUND):
        key_docs_ref[:, i * PAIR : (i + 1) * PAIR] = docs(positions((1, PAIR), 1, (z + step + ZS) % ZS))
    for copy in copies[:3]:
        copy.wait()
    kv_rows(own_ref, key_ref, value_ref, kv_ref, 0)


def own_kv(lengths, own, key_matrix, value_matrix):
    kind = jnp.bfloat16
    return pl.pallas_call(
        own_kv_kernel,
        in_specs=[HBM] * 4,
        out_specs=[VMEM] * 6,
        out_shape=[
            jax.ShapeDtypeStruct((ROWS, WIDTH), kind),
            jax.ShapeDtypeStruct((WIDTH, HEAD_SIZE), kind),
            jax.ShapeDtypeStruct((WIDTH, HEAD_SIZE), kind),
            jax.ShapeDtypeStruct((2 * PAIR, HEAD_SIZE), kind),
            jax.ShapeDtypeStruct((PAIR, 1), jnp.int32),
            jax.ShapeDtypeStruct((1, len(AROUND) * PAIR), jnp.int32),
        ],
        scratch_shapes=[pltpu.SMEM((16,), jnp.int32), pltpu.SemaphoreType.DMA((4,))],
        compiler_params=pltpu.CompilerParams(vmem_limit_bytes=52 * 2**20),
        cost_estimate=pl.CostEstimate(flops=2**27, bytes_accessed=2**21, transcendentals=0),
    )(lengths, own, key_matrix, value_matrix)


def other_kv_kernel(other_ref, key_ref, value_ref, held_ref, kv_ref):
    kv_rows(other_ref, key_ref, value_ref, kv_ref, ROWS)


def other_kv(other, key_mine, value_mine, kv):
    return pl.pallas_call(
        other_kv_kernel,
        in_specs=[VMEM] * 4,
        out_specs=VMEM,
        out_shape=jax.ShapeDtypeStruct(kv.shape, kv.dtype),
        input_output_aliases={3: 0},
        compiler_params=pltpu.CompilerParams(vmem_limit_bytes=8 * 2**20),
        cost_estimate=pl.CostEstimate(flops=2**27, bytes_accessed=2**21, transcendentals=0),
    )(other, key_mine, value_mine, kv)


def gate_kernel(*refs):
    pass


def gate(value, *after):
    return pl.pallas_call(
        gate_kernel,
        in_specs=[VMEM] * (1 + len(after)),
        out_specs=VMEM,
        out_shape=jax.ShapeDtypeStruct(value.shape, value.dtype),
        input_output_aliases={0: 0},
        compiler_params=pltpu.CompilerParams(vmem_limit_bytes=2**20),
    )(value, *after)


def pack_kernel(weight_ref, above_ref, below_ref, down_ref, up_ref):
    down_ref[:WIDTH] = weight_ref[...]
    down_ref[WIDTH:] = above_ref[...]
    up_ref[:WIDTH] = weight_ref[...]
    up_ref[WIDTH:] = below_ref[...]


def pack(weight, above, below):
    packed = jax.ShapeDtypeStruct((weight.shape[0] + above.shape[0], HEAD_SIZE), weight.dtype)
    return pl.pallas_call(
        pack_kernel,
        in_specs=[VMEM] * 3,
        out_specs=[VMEM] * 2,
        out_shape=[packed, packed],
        compiler_params=pltpu.CompilerParams(vmem_limit_bytes=4 * 2**20),
        cost_estimate=pl.CostEstimate(flops=2**32, bytes_accessed=2**21, transcendentals=0),
    )(weight, above, below)


def choose_kernel(first_ref, second_ref, out_ref):
    y, x, z, c = place()

    @pl.when(c == 0)
    def _():
        out_ref[...] = first_ref[...]

    @pl.when(c == 1)
    def _():
        out_ref[...] = second_ref[...]


def choose(first, second):
    return pl.pallas_call(
        choose_kernel,
        in_specs=[VMEM] * 2,
        out_specs=VMEM,
        out_shape=jax.ShapeDtypeStruct(first.shape, first.dtype),
        compiler_params=pltpu.CompilerParams(vmem_limit_bytes=4 * 2**20),
    )(first, second)


def attend(queries, kv, bases, docs, key_docs):
    factor = math.log2(math.e) / math.sqrt(HEAD_SIZE)
    scores = []
    for i in range(5):
        product = lax.dot_general(
            queries, kv[i][bases[i] : bases[i] + PAIR], (((1,), (1,)), ((), ())), preferred_element_type=jnp.float32
        )
        allowed = docs == key_docs[:, i * PAIR : (i + 1) * PAIR]
        scores.append(jnp.where(allowed, product, NEG))
    highest = functools.reduce(jnp.maximum, [jnp.max(s, axis=1, keepdims=True) for s in scores])
    summed, mixed = 0.0, 0.0
    for i in range(5):
        part = jnp.exp2((scores[i] - highest) * factor)
        summed = summed + jnp.sum(part, axis=1, keepdims=True)
        mixed = mixed + jnp.dot(
            part.astype(jnp.bfloat16), kv[i][bases[i] + PAIR : bases[i] + 2 * PAIR], preferred_element_type=jnp.float32
        )
    return (mixed / summed).astype(jnp.bfloat16)


def heads_kernel(shifts, bases, own_ref, other_ref, *refs):
    weights, refs = refs[: len(shifts)], refs[len(shifts) :]
    kv, (row_docs, key_docs, _, _, keep_ref, send_ref) = refs[:5], refs[5:]
    y, x, z, c = place()
    docs = row_docs[...]
    for first in range(0, len(shifts), 2):
        pair = weights[first : first + 2]
        matrix = jnp.concatenate([w[:WIDTH] for w in pair], axis=1)
        queries = jnp.concatenate(
            [
                jnp.dot(rows[...], matrix, preferred_element_type=jnp.float32).astype(jnp.bfloat16)
                for rows in (own_ref, other_ref)
            ],
            axis=0,
        )
        for i, shift in enumerate(shifts[first : first + 2]):
            color = (2 * x + 3 * y + z + shift) % 8
            slot = 0
            for k in range(8):
                slot = slot + jnp.where(color == k, jnp.where(c == 0, ORDER[0][k], ORDER[1][k]), 0)
            result = attend(queries[:, i * HEAD_SIZE : (i + 1) * HEAD_SIZE], kv, bases, docs, key_docs)
            columns = pl.ds(pl.multiple_of(slot * HEAD_SIZE, HEAD_SIZE), HEAD_SIZE)
            keep_ref[:, columns] = result[:ROWS]
            send_ref[:, columns] = result[ROWS:]


def some_heads(arrivals, own, other, kv, row_docs, key_docs, keep, send):
    inputs = [own, other, *(w for _, w in arrivals), *kv, row_docs, key_docs, keep, send]
    bases = [array.shape[0] - 2 * PAIR for array in kv]
    shape = jax.ShapeDtypeStruct(keep.shape, keep.dtype)
    return pl.pallas_call(
        functools.partial(heads_kernel, tuple(shift for shift, _ in arrivals), bases),
        in_specs=[VMEM] * len(inputs),
        out_specs=[VMEM, VMEM],
        out_shape=[shape, shape],
        input_output_aliases={len(inputs) - 2: 0, len(inputs) - 1: 1},
        compiler_params=pltpu.CompilerParams(vmem_limit_bytes=16 * 2**20),
        cost_estimate=pl.CostEstimate(flops=2**28, bytes_accessed=2**21, transcendentals=2**18),
    )(*inputs)


def join_kernel(mine_ref, other_ref, out_ref):
    y, x, z, c = place()
    out_ref[:, pl.ds(pl.multiple_of(c * HALF, HALF), HALF)] = mine_ref[...]
    out_ref[:, pl.ds(pl.multiple_of((1 - c) * HALF, HALF), HALF)] = other_ref[...]


def join(keep, arrived):
    return pl.pallas_call(
        join_kernel,
        grid=(1,),
        in_specs=[pl.BlockSpec((ROWS, HALF), lambda i: (0, 0))] * 2,
        out_specs=pl.BlockSpec((ROWS, 2 * HALF), lambda i: (0, 0)),
        out_shape=jax.ShapeDtypeStruct((ROWS, 2 * HALF), keep.dtype),
        compiler_params=pltpu.CompilerParams(vmem_limit_bytes=8 * 2**20),
    )(keep, arrived)


def body(tokens, query_weight, key_matrix, value_matrix, doc_lengths):
    weight = lax.ppermute(query_weight, AXES, first_moves())
    own, key_mine, value_mine, kv, row_docs, key_docs = own_kv(doc_lengths, tokens, key_matrix, value_matrix)
    other = swap_cores(tokens)
    kv = other_kv(other, key_mine, value_mine, kv)
    near = [lax.ppermute(kv, AXES, moves(lambda c, d=d: (0, 0, d))) for d in (1, -1)]

    weight = gate(weight, kv)
    right = lax.ppermute(weight, AXES, moves(lambda c: (0, 1, 0)))
    left = lax.ppermute(weight, AXES, moves(lambda c: (0, -1, 0)))
    down, up = pack(weight, *near)
    above = lax.ppermute(down, AXES, moves(lambda c: (0, 0, 1)))
    below = lax.ppermute(up, AXES, moves(lambda c: (0, 0, -1)))
    front = lax.ppermute(weight, AXES, moves(lambda c: (1, 0, 0)))
    back = lax.ppermute(weight, AXES, moves(lambda c: (-1, 0, 0)))
    across = lax.ppermute(choose(right, left), AXES, moves(lambda c: (0, 1, 0) if c == 0 else (0, -1, 0)))
    arrivals = [(0, weight), (2, right), (-2, left), (1, above), (-1, below), (3, front), (-3, back), (4, across)]
    kv_all = [kv, *near, above, below]

    keep = jnp.zeros((ROWS, HALF), jnp.bfloat16)
    send = jnp.zeros((ROWS, HALF), jnp.bfloat16)
    for some in (arrivals[:4], arrivals[4:6], arrivals[6:]):
        keep, send = some_heads(some, own, other, kv_all, row_docs, key_docs, keep, send)
    return join(keep, swap_cores(send))


def solution(mesh):
    in_specs = (P(("dp", "ctx"), None), P(None, "ctx"), P(), P(), P("dp"))
    out_specs = P(("dp", "ctx"), None)
    return jax.shard_map(body, mesh=mesh, in_specs=in_specs, out_specs=out_specs, check_vma=False)
```

```python
import functools
import math

import jax
import jax.numpy as jnp
from jax import lax
from jax.experimental import pallas as pl
from jax.experimental.pallas import tpu as pltpu
from jax.sharding import PartitionSpec as P

HEAD_SIZE = 128
WIDTH = 2048
ROWS = 128
PAIR = 2 * ROWS
HALF = 8 * HEAD_SIZE
NEG = -1e30

YS, XS, ZS, CORES = 8, 4, 8, 2
AXES = ("dp", "ctx")
ORDER = ((5, 3, 1, 7, 4, 2, 0, 6), (7, 3, 0, 6, 2, 4, 1, 5))
AROUND = (0, 1, -1, 2, -2)
VMEM = pl.BlockSpec(memory_space=pltpu.VMEM)
HBM = pl.BlockSpec(memory_space=pltpu.HBM)


def flat(y, x, z, c):
    return (((y % YS) * XS + x % XS) * ZS + z % ZS) * CORES + c


def everyone():
    return [(y, x, z, c) for y in range(YS) for x in range(XS) for z in range(ZS) for c in range(CORES)]


def first_moves():
    pairs = []
    for y, x, z, c in everyone():
        head = 8 * c + ORDER[c][(2 * x + 3 * y + z) % 8]
        pairs.append((flat(y, x, head // 2, head % 2), flat(y, x, z, c)))
    return pairs


def moves(step):
    pairs = []
    for y, x, z, c in everyone():
        dy, dx, dz = step(c)
        pairs.append((flat(y + dy, x + dx, z + dz, c), flat(y, x, z, c)))
    return pairs


def swap_cores(value):
    return lax.ppermute(value, AXES, [(flat(y, x, z, 1 - c), flat(y, x, z, c)) for y, x, z, c in everyone()])


def place():
    dp, ctx = lax.axis_index("dp"), lax.axis_index("ctx")
    return dp // XS, dp % XS, ctx // CORES, ctx % CORES


def kv_rows(rows, key_ref, value_ref, kv_ref, first):
    for base, matrix in ((0, key_ref), (PAIR, value_ref)):
        kv_ref[base + first : base + first + ROWS] = jnp.dot(
            rows[...], matrix[...], preferred_element_type=jnp.float32
        ).astype(jnp.bfloat16)


def own_kv_kernel(
    lengths_hbm, own_hbm, key_hbm, value_hbm, own_ref, key_ref, value_ref, kv_ref, row_docs_ref, key_docs_ref, lengths, sems
):
    y, x, z, c = place()
    mine = pl.ds(pl.multiple_of(c * HEAD_SIZE, HEAD_SIZE), HEAD_SIZE)
    copies = [
        pltpu.make_async_copy(own_hbm, own_ref, sems.at[0]),
        pltpu.make_async_copy(key_hbm.at[:, mine], key_ref, sems.at[1]),
        pltpu.make_async_copy(value_hbm.at[:, mine], value_ref, sems.at[2]),
        pltpu.make_async_copy(lengths_hbm, lengths, sems.at[3]),
    ]
    for copy in copies:
        copy.start()

    def positions(shape, axis, block):
        row = lax.broadcasted_iota(jnp.int32, shape, axis)
        return jnp.where(row < ROWS, row + ROWS * c, row - ROWS * c) + PAIR * block

    def docs(place_in_group):
        end = 0
        total = jnp.zeros(place_in_group.shape, jnp.int32)
        for e in range(16):
            end = end + lengths[e]
            total = total + (place_in_group >= end).astype(jnp.int32)
        return total

    copies[3].wait()
    row_docs_ref[...] = docs(positions((PAIR, 1), 0, z))
    for i, step in enumerate(AROUND):
        key_docs_ref[:, i * PAIR : (i + 1) * PAIR] = docs(positions((1, PAIR), 1, (z + step + ZS) % ZS))
    for copy in copies[:3]:
        copy.wait()
    kv_rows(own_ref, key_ref, value_ref, kv_ref, 0)


def own_kv(lengths, own, key_matrix, value_matrix):
    kind = jnp.bfloat16
    return pl.pallas_call(
        own_kv_kernel,
        in_specs=[HBM] * 4,
        out_specs=[VMEM] * 6,
        out_shape=[
            jax.ShapeDtypeStruct((ROWS, WIDTH), kind),
            jax.ShapeDtypeStruct((WIDTH, HEAD_SIZE), kind),
            jax.ShapeDtypeStruct((WIDTH, HEAD_SIZE), kind),
            jax.ShapeDtypeStruct((2 * PAIR, HEAD_SIZE), kind),
            jax.ShapeDtypeStruct((PAIR, 1), jnp.int32),
            jax.ShapeDtypeStruct((1, len(AROUND) * PAIR), jnp.int32),
        ],
        scratch_shapes=[pltpu.SMEM((16,), jnp.int32), pltpu.SemaphoreType.DMA((4,))],
        compiler_params=pltpu.CompilerParams(vmem_limit_bytes=52 * 2**20),
        cost_estimate=pl.CostEstimate(flops=2**27, bytes_accessed=2**21, transcendentals=0),
    )(lengths, own, key_matrix, value_matrix)


def other_kv_kernel(other_ref, key_ref, value_ref, held_ref, kv_ref):
    kv_rows(other_ref, key_ref, value_ref, kv_ref, ROWS)


def other_kv(other, key_mine, value_mine, kv):
    return pl.pallas_call(
        other_kv_kernel,
        in_specs=[VMEM] * 4,
        out_specs=VMEM,
        out_shape=jax.ShapeDtypeStruct(kv.shape, kv.dtype),
        input_output_aliases={3: 0},
        compiler_params=pltpu.CompilerParams(vmem_limit_bytes=8 * 2**20),
        cost_estimate=pl.CostEstimate(flops=2**27, bytes_accessed=2**21, transcendentals=0),
    )(other, key_mine, value_mine, kv)


def gate_kernel(*refs):
    pass


def gate(value, *after):
    return pl.pallas_call(
        gate_kernel,
        in_specs=[VMEM] * (1 + len(after)),
        out_specs=VMEM,
        out_shape=jax.ShapeDtypeStruct(value.shape, value.dtype),
        input_output_aliases={0: 0},
        compiler_params=pltpu.CompilerParams(vmem_limit_bytes=2**20),
    )(value, *after)


def pack_kernel(weight_ref, above_ref, below_ref, down_ref, up_ref):
    down_ref[:WIDTH] = weight_ref[...]
    down_ref[WIDTH:] = above_ref[...]
    up_ref[:WIDTH] = weight_ref[...]
    up_ref[WIDTH:] = below_ref[...]


def pack(weight, above, below):
    packed = jax.ShapeDtypeStruct((weight.shape[0] + above.shape[0], HEAD_SIZE), weight.dtype)
    return pl.pallas_call(
        pack_kernel,
        in_specs=[VMEM] * 3,
        out_specs=[VMEM] * 2,
        out_shape=[packed, packed],
        compiler_params=pltpu.CompilerParams(vmem_limit_bytes=4 * 2**20),
        cost_estimate=pl.CostEstimate(flops=2**32, bytes_accessed=2**21, transcendentals=0),
    )(weight, above, below)


def choose_kernel(first_ref, second_ref, out_ref):
    y, x, z, c = place()

    @pl.when(c == 0)
    def _():
        out_ref[...] = first_ref[...]

    @pl.when(c == 1)
    def _():
        out_ref[...] = second_ref[...]


def choose(first, second):
    return pl.pallas_call(
        choose_kernel,
        in_specs=[VMEM] * 2,
        out_specs=VMEM,
        out_shape=jax.ShapeDtypeStruct(first.shape, first.dtype),
        compiler_params=pltpu.CompilerParams(vmem_limit_bytes=4 * 2**20),
    )(first, second)


def attend(queries, kv, bases, docs, key_docs, blocks):
    factor = math.log2(math.e) / math.sqrt(HEAD_SIZE)
    scores = {}
    for i in blocks:
        product = lax.dot_general(
            queries, kv[i][bases[i] : bases[i] + PAIR], (((1,), (1,)), ((), ())), preferred_element_type=jnp.float32
        )
        allowed = docs == key_docs[:, i * PAIR : (i + 1) * PAIR]
        scores[i] = jnp.where(allowed, product, NEG)
    highest = functools.reduce(jnp.maximum, [jnp.max(s, axis=1, keepdims=True) for s in scores.values()])
    summed, mixed = 0.0, 0.0
    for i in blocks:
        part = jnp.exp2((scores[i] - highest) * factor)
        summed = summed + jnp.sum(part, axis=1, keepdims=True)
        mixed = mixed + jnp.dot(
            part.astype(jnp.bfloat16), kv[i][bases[i] + PAIR : bases[i] + 2 * PAIR], preferred_element_type=jnp.float32
        )
    return (mixed / summed).astype(jnp.bfloat16)


def heads_kernel(shifts, bases, own_ref, other_ref, *refs):
    weights, refs = refs[: len(shifts)], refs[len(shifts) :]
    kv, (row_docs, key_docs, _, _, keep_ref, send_ref) = refs[:5], refs[5:]
    y, x, z, c = place()
    docs = row_docs[...]
    queries = []
    for first in range(0, len(shifts), 2):
        matrix = jnp.concatenate([w[:WIDTH] for w in weights[first : first + 2]], axis=1)
        queries.append(
            jnp.concatenate(
                [
                    jnp.dot(rows[...], matrix, preferred_element_type=jnp.float32).astype(jnp.bfloat16)
                    for rows in (own_ref, other_ref)
                ],
                axis=0,
            )
        )

    lowest = jnp.minimum(row_docs[0, 0], row_docs[ROWS, 0])
    highest = jnp.maximum(row_docs[ROWS - 1, 0], row_docs[PAIR - 1, 0])

    def reached(i):
        first = jnp.minimum(key_docs[0, i * PAIR], key_docs[0, i * PAIR + ROWS])
        last = jnp.maximum(key_docs[0, i * PAIR + ROWS - 1], key_docs[0, i * PAIR + PAIR - 1])
        return jnp.logical_and(first <= highest, last >= lowest)

    after, before = reached(3), reached(4)
    cases = (
        (jnp.logical_not(jnp.logical_or(after, before)), (0, 1, 2)),
        (jnp.logical_and(after, jnp.logical_not(before)), (0, 1, 2, 3)),
        (jnp.logical_and(before, jnp.logical_not(after)), (0, 1, 2, 4)),
        (jnp.logical_and(after, before), (0, 1, 2, 3, 4)),
    )
    for case, blocks in cases:

        @pl.when(case)
        def _(blocks=blocks):
            for n, shift in enumerate(shifts):
                color = (2 * x + 3 * y + z + shift) % 8
                slot = 0
                for k in range(8):
                    slot = slot + jnp.where(color == k, jnp.where(c == 0, ORDER[0][k], ORDER[1][k]), 0)
                half = queries[n // 2][:, n % 2 * HEAD_SIZE : (n % 2 + 1) * HEAD_SIZE]
                result = attend(half, kv, bases, docs, key_docs, blocks)
                columns = pl.ds(pl.multiple_of(slot * HEAD_SIZE, HEAD_SIZE), HEAD_SIZE)
                keep_ref[:, columns] = result[:ROWS]
                send_ref[:, columns] = result[ROWS:]


def some_heads(arrivals, own, other, kv, row_docs, key_docs, keep, send):
    inputs = [own, other, *(w for _, w in arrivals), *kv, row_docs, key_docs, keep, send]
    bases = [array.shape[0] - 2 * PAIR for array in kv]
    shape = jax.ShapeDtypeStruct(keep.shape, keep.dtype)
    return pl.pallas_call(
        functools.partial(heads_kernel, tuple(shift for shift, _ in arrivals), bases),
        in_specs=[VMEM] * len(inputs),
        out_specs=[VMEM, VMEM],
        out_shape=[shape, shape],
        input_output_aliases={len(inputs) - 2: 0, len(inputs) - 1: 1},
        compiler_params=pltpu.CompilerParams(vmem_limit_bytes=16 * 2**20),
        cost_estimate=pl.CostEstimate(flops=2**28, bytes_accessed=2**21, transcendentals=2**18),
    )(*inputs)


def join_kernel(mine_ref, other_ref, out_ref):
    y, x, z, c = place()
    out_ref[:, pl.ds(pl.multiple_of(c * HALF, HALF), HALF)] = mine_ref[...]
    out_ref[:, pl.ds(pl.multiple_of((1 - c) * HALF, HALF), HALF)] = other_ref[...]


def join(keep, arrived):
    return pl.pallas_call(
        join_kernel,
        grid=(1,),
        in_specs=[pl.BlockSpec((ROWS, HALF), lambda i: (0, 0))] * 2,
        out_specs=pl.BlockSpec((ROWS, 2 * HALF), lambda i: (0, 0)),
        out_shape=jax.ShapeDtypeStruct((ROWS, 2 * HALF), keep.dtype),
        compiler_params=pltpu.CompilerParams(vmem_limit_bytes=8 * 2**20),
    )(keep, arrived)


def body(tokens, query_weight, key_matrix, value_matrix, doc_lengths):
    weight = lax.ppermute(query_weight, AXES, first_moves())
    own, key_mine, value_mine, kv, row_docs, key_docs = own_kv(doc_lengths, tokens, key_matrix, value_matrix)
    other = swap_cores(tokens)
    kv = other_kv(other, key_mine, value_mine, kv)
    near = [lax.ppermute(kv, AXES, moves(lambda c, d=d: (0, 0, d))) for d in (1, -1)]

    weight = gate(weight, kv)
    right = lax.ppermute(weight, AXES, moves(lambda c: (0, 1, 0)))
    left = lax.ppermute(weight, AXES, moves(lambda c: (0, -1, 0)))
    down, up = pack(weight, *near)
    above = lax.ppermute(down, AXES, moves(lambda c: (0, 0, 1)))
    below = lax.ppermute(up, AXES, moves(lambda c: (0, 0, -1)))
    front = lax.ppermute(weight, AXES, moves(lambda c: (1, 0, 0)))
    back = lax.ppermute(weight, AXES, moves(lambda c: (-1, 0, 0)))
    across = lax.ppermute(choose(right, left), AXES, moves(lambda c: (0, 1, 0) if c == 0 else (0, -1, 0)))
    arrivals = [(0, weight), (2, right), (-2, left), (1, above), (-1, below), (3, front), (-3, back), (4, across)]
    kv_all = [kv, *near, above, below]

    keep = jnp.zeros((ROWS, HALF), jnp.bfloat16)
    send = jnp.zeros((ROWS, HALF), jnp.bfloat16)
    for some in (arrivals[:4], arrivals[4:6], arrivals[6:]):
        keep, send = some_heads(some, own, other, kv_all, row_docs, key_docs, keep, send)
    return join(keep, swap_cores(send))


def solution(mesh):
    in_specs = (P(("dp", "ctx"), None), P(None, "ctx"), P(), P(), P("dp"))
    out_specs = P(("dp", "ctx"), None)
    return jax.shard_map(body, mesh=mesh, in_specs=in_specs, out_specs=out_specs, check_vma=False)
```

```python
import functools
import math

import jax
import jax.numpy as jnp
from jax import lax
from jax.experimental import pallas as pl
from jax.experimental.pallas import tpu as pltpu
from jax.sharding import PartitionSpec as P

HEAD_SIZE = 128
WIDTH = 2048
ROWS = 128
PAIR = 2 * ROWS
HALF = 8 * HEAD_SIZE
NEG = -1e30

YS, XS, ZS, CORES = 8, 4, 8, 2
AXES = ("dp", "ctx")
ORDER = ((5, 3, 1, 7, 4, 2, 0, 6), (7, 3, 0, 6, 2, 4, 1, 5))
AROUND = (0, 1, -1, 2, -2)
VMEM = pl.BlockSpec(memory_space=pltpu.VMEM)
HBM = pl.BlockSpec(memory_space=pltpu.HBM)


def flat(y, x, z, c):
    return (((y % YS) * XS + x % XS) * ZS + z % ZS) * CORES + c


def everyone():
    return [(y, x, z, c) for y in range(YS) for x in range(XS) for z in range(ZS) for c in range(CORES)]


def first_moves():
    pairs = []
    for y, x, z, c in everyone():
        head = 8 * c + ORDER[c][(2 * x + 3 * y + z) % 8]
        pairs.append((flat(y, x, head // 2, head % 2), flat(y, x, z, c)))
    return pairs


def moves(step):
    pairs = []
    for y, x, z, c in everyone():
        dy, dx, dz = step(c)
        pairs.append((flat(y + dy, x + dx, z + dz, c), flat(y, x, z, c)))
    return pairs


def swap_cores(value):
    return lax.ppermute(value, AXES, [(flat(y, x, z, 1 - c), flat(y, x, z, c)) for y, x, z, c in everyone()])


def place():
    dp, ctx = lax.axis_index("dp"), lax.axis_index("ctx")
    return dp // XS, dp % XS, ctx // CORES, ctx % CORES


def kv_rows(rows, key_ref, value_ref, kv_ref, first):
    for base, matrix in ((0, key_ref), (PAIR, value_ref)):
        kv_ref[base + first : base + first + ROWS] = jnp.dot(
            rows[...], matrix[...], preferred_element_type=jnp.float32
        ).astype(jnp.bfloat16)


def own_kv_kernel(
    lengths_hbm, own_hbm, key_hbm, value_hbm, own_ref, key_ref, value_ref, kv_ref, row_docs_ref, key_docs_ref, lengths, sems
):
    y, x, z, c = place()
    mine = pl.ds(pl.multiple_of(c * HEAD_SIZE, HEAD_SIZE), HEAD_SIZE)
    copies = [
        pltpu.make_async_copy(own_hbm, own_ref, sems.at[0]),
        pltpu.make_async_copy(key_hbm.at[:, mine], key_ref, sems.at[1]),
        pltpu.make_async_copy(value_hbm.at[:, mine], value_ref, sems.at[2]),
        pltpu.make_async_copy(lengths_hbm, lengths, sems.at[3]),
    ]
    for copy in copies:
        copy.start()

    def positions(shape, axis, block):
        row = lax.broadcasted_iota(jnp.int32, shape, axis)
        return jnp.where(row < ROWS, row + ROWS * c, row - ROWS * c) + PAIR * block

    def docs(place_in_group):
        end = 0
        total = jnp.zeros(place_in_group.shape, jnp.int32)
        for e in range(16):
            end = end + lengths[e]
            total = total + (place_in_group >= end).astype(jnp.int32)
        return total

    copies[3].wait()
    row_docs_ref[...] = docs(positions((PAIR, 1), 0, z))
    for i, step in enumerate(AROUND):
        key_docs_ref[:, i * PAIR : (i + 1) * PAIR] = docs(positions((1, PAIR), 1, (z + step + ZS) % ZS))
    for copy in copies[:3]:
        copy.wait()
    kv_rows(own_ref, key_ref, value_ref, kv_ref, 0)


def own_kv(lengths, own, key_matrix, value_matrix):
    kind = jnp.bfloat16
    return pl.pallas_call(
        own_kv_kernel,
        in_specs=[HBM] * 4,
        out_specs=[VMEM] * 6,
        out_shape=[
            jax.ShapeDtypeStruct((ROWS, WIDTH), kind),
            jax.ShapeDtypeStruct((WIDTH, HEAD_SIZE), kind),
            jax.ShapeDtypeStruct((WIDTH, HEAD_SIZE), kind),
            jax.ShapeDtypeStruct((2 * PAIR, HEAD_SIZE), kind),
            jax.ShapeDtypeStruct((PAIR, 1), jnp.int32),
            jax.ShapeDtypeStruct((1, len(AROUND) * PAIR), jnp.int32),
        ],
        scratch_shapes=[pltpu.SMEM((16,), jnp.int32), pltpu.SemaphoreType.DMA((4,))],
        compiler_params=pltpu.CompilerParams(vmem_limit_bytes=52 * 2**20),
        cost_estimate=pl.CostEstimate(flops=2**27, bytes_accessed=2**21, transcendentals=0),
    )(lengths, own, key_matrix, value_matrix)


def other_kv_kernel(other_ref, key_ref, value_ref, held_ref, kv_ref):
    kv_rows(other_ref, key_ref, value_ref, kv_ref, ROWS)


def other_kv(other, key_mine, value_mine, kv):
    return pl.pallas_call(
        other_kv_kernel,
        in_specs=[VMEM] * 4,
        out_specs=VMEM,
        out_shape=jax.ShapeDtypeStruct(kv.shape, kv.dtype),
        input_output_aliases={3: 0},
        compiler_params=pltpu.CompilerParams(vmem_limit_bytes=8 * 2**20),
        cost_estimate=pl.CostEstimate(flops=2**27, bytes_accessed=2**21, transcendentals=0),
    )(other, key_mine, value_mine, kv)


def gate_kernel(*refs):
    pass


def gate(value, *after):
    return pl.pallas_call(
        gate_kernel,
        in_specs=[VMEM] * (1 + len(after)),
        out_specs=VMEM,
        out_shape=jax.ShapeDtypeStruct(value.shape, value.dtype),
        input_output_aliases={0: 0},
        compiler_params=pltpu.CompilerParams(vmem_limit_bytes=2**20),
    )(value, *after)


def pack_kernel(weight_ref, above_ref, below_ref, down_ref, up_ref):
    down_ref[:WIDTH] = weight_ref[...]
    down_ref[WIDTH:] = above_ref[...]
    up_ref[:WIDTH] = weight_ref[...]
    up_ref[WIDTH:] = below_ref[...]


def pack(weight, above, below):
    packed = jax.ShapeDtypeStruct((weight.shape[0] + above.shape[0], HEAD_SIZE), weight.dtype)
    return pl.pallas_call(
        pack_kernel,
        in_specs=[VMEM] * 3,
        out_specs=[VMEM] * 2,
        out_shape=[packed, packed],
        compiler_params=pltpu.CompilerParams(vmem_limit_bytes=4 * 2**20),
        cost_estimate=pl.CostEstimate(flops=2**32, bytes_accessed=2**21, transcendentals=0),
    )(weight, above, below)


def choose_kernel(first_ref, second_ref, out_ref):
    y, x, z, c = place()

    @pl.when(c == 0)
    def _():
        out_ref[...] = first_ref[...]

    @pl.when(c == 1)
    def _():
        out_ref[...] = second_ref[...]


def choose(first, second):
    return pl.pallas_call(
        choose_kernel,
        in_specs=[VMEM] * 2,
        out_specs=VMEM,
        out_shape=jax.ShapeDtypeStruct(first.shape, first.dtype),
        compiler_params=pltpu.CompilerParams(vmem_limit_bytes=4 * 2**20),
    )(first, second)


def attend(queries, kv, bases, docs, key_docs, blocks):
    factor = math.log2(math.e) / math.sqrt(HEAD_SIZE)
    scores = {}
    for i in blocks:
        product = lax.dot_general(
            queries, kv[i][bases[i] : bases[i] + PAIR], (((1,), (1,)), ((), ())), preferred_element_type=jnp.float32
        )
        allowed = docs == key_docs[:, i * PAIR : (i + 1) * PAIR]
        scores[i] = jnp.where(allowed, product, NEG)
    highest = functools.reduce(jnp.maximum, [jnp.max(s, axis=1, keepdims=True) for s in scores.values()])
    summed, mixed = 0.0, 0.0
    for i in blocks:
        part = jnp.exp2((scores[i] - highest) * factor)
        summed = summed + jnp.sum(part, axis=1, keepdims=True)
        mixed = mixed + jnp.dot(
            part.astype(jnp.bfloat16), kv[i][bases[i] + PAIR : bases[i] + 2 * PAIR], preferred_element_type=jnp.float32
        )
    return (mixed / summed).astype(jnp.bfloat16)


def heads_kernel(shifts, bases, own_ref, other_ref, *refs):
    weights, refs = refs[: len(shifts)], refs[len(shifts) :]
    kv, (row_docs, key_docs, _, _, keep_ref, send_ref) = refs[:5], refs[5:]
    y, x, z, c = place()
    docs = row_docs[...]
    queries = []
    for first in range(0, len(shifts), 2):
        matrix = jnp.concatenate([w[:WIDTH] for w in weights[first : first + 2]], axis=1)
        queries.append(
            jnp.concatenate(
                [
                    jnp.dot(rows[...], matrix, preferred_element_type=jnp.float32).astype(jnp.bfloat16)
                    for rows in (own_ref, other_ref)
                ],
                axis=0,
            )
        )

    lowest = jnp.minimum(row_docs[0, 0], row_docs[ROWS, 0])
    highest = jnp.maximum(row_docs[ROWS - 1, 0], row_docs[PAIR - 1, 0])

    def reached(i):
        first = jnp.minimum(key_docs[0, i * PAIR], key_docs[0, i * PAIR + ROWS])
        last = jnp.maximum(key_docs[0, i * PAIR + ROWS - 1], key_docs[0, i * PAIR + PAIR - 1])
        return jnp.logical_and(first <= highest, last >= lowest)

    after, before = reached(3), reached(4)
    cases = (
        (jnp.logical_not(jnp.logical_or(after, before)), (0, 1, 2)),
        (jnp.logical_and(after, jnp.logical_not(before)), (0, 1, 2, 3)),
        (jnp.logical_and(before, jnp.logical_not(after)), (0, 1, 2, 4)),
        (jnp.logical_and(after, before), (0, 1, 2, 3, 4)),
    )
    for case, blocks in cases:

        @pl.when(case)
        def _(blocks=blocks):
            for n, shift in enumerate(shifts):
                color = (2 * x + 3 * y + z + shift) % 8
                slot = 0
                for k in range(8):
                    slot = slot + jnp.where(color == k, jnp.where(c == 0, ORDER[0][k], ORDER[1][k]), 0)
                half = queries[n // 2][:, n % 2 * HEAD_SIZE : (n % 2 + 1) * HEAD_SIZE]
                result = attend(half, kv, bases, docs, key_docs, blocks)
                columns = pl.ds(pl.multiple_of(slot * HEAD_SIZE, HEAD_SIZE), HEAD_SIZE)
                keep_ref[:, columns] = result[:ROWS]
                send_ref[:, columns] = result[ROWS:]


def some_heads(arrivals, own, other, kv, row_docs, key_docs, keep, send):
    inputs = [own, other, *(w for _, w in arrivals), *kv, row_docs, key_docs, keep, send]
    bases = [array.shape[0] - 2 * PAIR for array in kv]
    shape = jax.ShapeDtypeStruct(keep.shape, keep.dtype)
    return pl.pallas_call(
        functools.partial(heads_kernel, tuple(shift for shift, _ in arrivals), bases),
        in_specs=[VMEM] * len(inputs),
        out_specs=[VMEM, VMEM],
        out_shape=[shape, shape],
        input_output_aliases={len(inputs) - 2: 0, len(inputs) - 1: 1},
        compiler_params=pltpu.CompilerParams(vmem_limit_bytes=16 * 2**20),
        cost_estimate=pl.CostEstimate(flops=2**28, bytes_accessed=2**21, transcendentals=2**18),
    )(*inputs)


def put_kernel(side, value_ref, *refs):
    out_ref, sem = refs[-2:]
    y, x, z, c = place()
    core = c if side == 0 else 1 - c
    columns = pl.ds(pl.multiple_of(core * HALF, HALF), HALF)
    copy = pltpu.make_async_copy(value_ref, out_ref.at[:, columns], sem)
    copy.start()
    copy.wait()


def put(side, value, result=None):
    inputs = [value] if result is None else [value, result]
    return pl.pallas_call(
        functools.partial(put_kernel, side),
        in_specs=[VMEM, HBM][: len(inputs)],
        out_specs=HBM,
        out_shape=jax.ShapeDtypeStruct((ROWS, 2 * HALF), value.dtype),
        scratch_shapes=[pltpu.SemaphoreType.DMA],
        input_output_aliases={} if result is None else {1: 0},
        compiler_params=pltpu.CompilerParams(vmem_limit_bytes=2**20),
        cost_estimate=pl.CostEstimate(flops=2**24, bytes_accessed=2**18, transcendentals=0),
    )(*inputs)


def body(tokens, query_weight, key_matrix, value_matrix, doc_lengths):
    weight = lax.ppermute(query_weight, AXES, first_moves())
    own, key_mine, value_mine, kv, row_docs, key_docs = own_kv(doc_lengths, tokens, key_matrix, value_matrix)
    other = swap_cores(tokens)
    kv = other_kv(other, key_mine, value_mine, kv)
    near = [lax.ppermute(kv, AXES, moves(lambda c, d=d: (0, 0, d))) for d in (1, -1)]

    weight = gate(weight, kv)
    right = lax.ppermute(weight, AXES, moves(lambda c: (0, 1, 0)))
    left = lax.ppermute(weight, AXES, moves(lambda c: (0, -1, 0)))
    down, up = pack(weight, *near)
    above = lax.ppermute(down, AXES, moves(lambda c: (0, 0, 1)))
    below = lax.ppermute(up, AXES, moves(lambda c: (0, 0, -1)))
    front = lax.ppermute(weight, AXES, moves(lambda c: (1, 0, 0)))
    back = lax.ppermute(weight, AXES, moves(lambda c: (-1, 0, 0)))
    across = lax.ppermute(choose(right, left), AXES, moves(lambda c: (0, 1, 0) if c == 0 else (0, -1, 0)))
    arrivals = [(0, weight), (2, right), (-2, left), (1, above), (-1, below), (3, front), (-3, back), (4, across)]
    kv_all = [kv, *near, above, below]

    keep = jnp.zeros((ROWS, HALF), jnp.bfloat16)
    send = jnp.zeros((ROWS, HALF), jnp.bfloat16)
    for some in (arrivals[:4], arrivals[4:7], arrivals[7:]):
        keep, send = some_heads(some, own, other, kv_all, row_docs, key_docs, keep, send)
    return put(1, swap_cores(send), put(0, keep))


def solution(mesh):
    in_specs = (P(("dp", "ctx"), None), P(None, "ctx"), P(), P(), P("dp"))
    out_specs = P(("dp", "ctx"), None)
    return jax.shard_map(body, mesh=mesh, in_specs=in_specs, out_specs=out_specs, check_vma=False)
```

```python
import functools
import math

import jax
import jax.numpy as jnp
from jax import lax
from jax.experimental import pallas as pl
from jax.experimental.pallas import tpu as pltpu
from jax.sharding import PartitionSpec as P

HEAD_SIZE = 128
WIDTH = 2048
ROWS = 128
PAIR = 2 * ROWS
HALF = 8 * HEAD_SIZE
NEG = -1e30

YS, XS, ZS, CORES = 8, 4, 8, 2
AXES = ("dp", "ctx")
ORDER = ((0, 6, 4, 2, 1, 7, 5, 3), (1, 7, 5, 3, 0, 6, 4, 2))
AROUND = (0, 1, -1, 2, -2)
VMEM = pl.BlockSpec(memory_space=pltpu.VMEM)
HBM = pl.BlockSpec(memory_space=pltpu.HBM)


def flat(y, x, z, c):
    return (((y % YS) * XS + x % XS) * ZS + z % ZS) * CORES + c


def everyone():
    return [(y, x, z, c) for y in range(YS) for x in range(XS) for z in range(ZS) for c in range(CORES)]


def first_moves():
    pairs = []
    for y, x, z, c in everyone():
        head = 8 * c + ORDER[c][(2 * x + 3 * y + z) % 8]
        pairs.append((flat(y, x, head // 2, head % 2), flat(y, x, z, c)))
    return pairs


def moves(step):
    pairs = []
    for y, x, z, c in everyone():
        dy, dx, dz = step(c)
        pairs.append((flat(y + dy, x + dx, z + dz, c), flat(y, x, z, c)))
    return pairs


def swap_cores(value):
    return lax.ppermute(value, AXES, [(flat(y, x, z, 1 - c), flat(y, x, z, c)) for y, x, z, c in everyone()])


def place():
    dp, ctx = lax.axis_index("dp"), lax.axis_index("ctx")
    return dp // XS, dp % XS, ctx // CORES, ctx % CORES


def kv_rows(rows, key_ref, value_ref, kv_ref, first):
    for base, matrix in ((0, key_ref), (PAIR, value_ref)):
        kv_ref[base + first : base + first + ROWS] = jnp.dot(
            rows[...], matrix[...], preferred_element_type=jnp.float32
        ).astype(jnp.bfloat16)


def own_kv_kernel(
    lengths_hbm, own_hbm, key_hbm, value_hbm, own_ref, key_ref, value_ref, kv_ref, row_docs_ref, key_docs_ref, lengths, sems
):
    y, x, z, c = place()
    mine = pl.ds(pl.multiple_of(c * HEAD_SIZE, HEAD_SIZE), HEAD_SIZE)
    copies = [
        pltpu.make_async_copy(own_hbm, own_ref, sems.at[0]),
        pltpu.make_async_copy(key_hbm.at[:, mine], key_ref, sems.at[1]),
        pltpu.make_async_copy(value_hbm.at[:, mine], value_ref, sems.at[2]),
        pltpu.make_async_copy(lengths_hbm, lengths, sems.at[3]),
    ]
    for copy in copies:
        copy.start()

    def positions(shape, axis, block):
        row = lax.broadcasted_iota(jnp.int32, shape, axis)
        return jnp.where(row < ROWS, row + ROWS * c, row - ROWS * c) + PAIR * block

    def docs(place_in_group):
        end = 0
        total = jnp.zeros(place_in_group.shape, jnp.int32)
        for e in range(16):
            end = end + lengths[e]
            total = total + (place_in_group >= end).astype(jnp.int32)
        return total

    copies[3].wait()
    row_docs_ref[...] = docs(positions((PAIR, 1), 0, z))
    for i, step in enumerate(AROUND):
        key_docs_ref[:, i * PAIR : (i + 1) * PAIR] = docs(positions((1, PAIR), 1, (z + step + ZS) % ZS))
    for copy in copies[:3]:
        copy.wait()
    kv_rows(own_ref, key_ref, value_ref, kv_ref, 0)


def own_kv(lengths, own, key_matrix, value_matrix):
    kind = jnp.bfloat16
    return pl.pallas_call(
        own_kv_kernel,
        in_specs=[HBM] * 4,
        out_specs=[VMEM] * 6,
        out_shape=[
            jax.ShapeDtypeStruct((ROWS, WIDTH), kind),
            jax.ShapeDtypeStruct((WIDTH, HEAD_SIZE), kind),
            jax.ShapeDtypeStruct((WIDTH, HEAD_SIZE), kind),
            jax.ShapeDtypeStruct((2 * PAIR, HEAD_SIZE), kind),
            jax.ShapeDtypeStruct((PAIR, 1), jnp.int32),
            jax.ShapeDtypeStruct((1, len(AROUND) * PAIR), jnp.int32),
        ],
        scratch_shapes=[pltpu.SMEM((16,), jnp.int32), pltpu.SemaphoreType.DMA((4,))],
        compiler_params=pltpu.CompilerParams(vmem_limit_bytes=52 * 2**20),
        cost_estimate=pl.CostEstimate(flops=2**27, bytes_accessed=2**21, transcendentals=0),
    )(lengths, own, key_matrix, value_matrix)


def other_kv_kernel(other_ref, key_ref, value_ref, held_ref, kv_ref):
    kv_rows(other_ref, key_ref, value_ref, kv_ref, ROWS)


def other_kv(other, key_mine, value_mine, kv):
    return pl.pallas_call(
        other_kv_kernel,
        in_specs=[VMEM] * 4,
        out_specs=VMEM,
        out_shape=jax.ShapeDtypeStruct(kv.shape, kv.dtype),
        input_output_aliases={3: 0},
        compiler_params=pltpu.CompilerParams(vmem_limit_bytes=8 * 2**20),
        cost_estimate=pl.CostEstimate(flops=2**27, bytes_accessed=2**21, transcendentals=0),
    )(other, key_mine, value_mine, kv)


def gate_kernel(*refs):
    pass


def gate(value, *after):
    return pl.pallas_call(
        gate_kernel,
        in_specs=[VMEM] * (1 + len(after)),
        out_specs=VMEM,
        out_shape=jax.ShapeDtypeStruct(value.shape, value.dtype),
        input_output_aliases={0: 0},
        compiler_params=pltpu.CompilerParams(vmem_limit_bytes=2**20),
    )(value, *after)


def pack_kernel(weight_ref, above_ref, below_ref, down_ref, up_ref):
    down_ref[:WIDTH] = weight_ref[...]
    down_ref[WIDTH:] = above_ref[...]
    up_ref[:WIDTH] = weight_ref[...]
    up_ref[WIDTH:] = below_ref[...]


def pack(weight, above, below):
    packed = jax.ShapeDtypeStruct((weight.shape[0] + above.shape[0], HEAD_SIZE), weight.dtype)
    return pl.pallas_call(
        pack_kernel,
        in_specs=[VMEM] * 3,
        out_specs=[VMEM] * 2,
        out_shape=[packed, packed],
        compiler_params=pltpu.CompilerParams(vmem_limit_bytes=4 * 2**20),
        cost_estimate=pl.CostEstimate(flops=2**32, bytes_accessed=2**21, transcendentals=0),
    )(weight, above, below)


def choose_kernel(first_ref, second_ref, out_ref):
    y, x, z, c = place()

    @pl.when(c == 0)
    def _():
        out_ref[...] = first_ref[...]

    @pl.when(c == 1)
    def _():
        out_ref[...] = second_ref[...]


def choose(first, second):
    return pl.pallas_call(
        choose_kernel,
        in_specs=[VMEM] * 2,
        out_specs=VMEM,
        out_shape=jax.ShapeDtypeStruct(first.shape, first.dtype),
        compiler_params=pltpu.CompilerParams(vmem_limit_bytes=4 * 2**20),
    )(first, second)


def attend(queries, kv, bases, docs, key_docs, blocks):
    factor = math.log2(math.e) / math.sqrt(HEAD_SIZE)
    scores = {}
    for i in blocks:
        product = lax.dot_general(
            queries, kv[i][bases[i] : bases[i] + PAIR], (((1,), (1,)), ((), ())), preferred_element_type=jnp.float32
        )
        allowed = docs == key_docs[:, i * PAIR : (i + 1) * PAIR]
        scores[i] = jnp.where(allowed, product, NEG)
    highest = functools.reduce(jnp.maximum, [jnp.max(s, axis=1, keepdims=True) for s in scores.values()])
    summed, mixed = 0.0, 0.0
    for i in blocks:
        part = jnp.exp2((scores[i] - highest) * factor)
        summed = summed + jnp.sum(part, axis=1, keepdims=True)
        mixed = mixed + jnp.dot(
            part.astype(jnp.bfloat16), kv[i][bases[i] + PAIR : bases[i] + 2 * PAIR], preferred_element_type=jnp.float32
        )
    return (mixed / summed).astype(jnp.bfloat16)


def heads_kernel(shifts, bases, own_ref, other_ref, *refs):
    weights, refs = refs[: len(shifts)], refs[len(shifts) :]
    kv, (row_docs, key_docs, _, _, keep_ref, send_ref) = refs[:5], refs[5:]
    y, x, z, c = place()
    docs = row_docs[...]
    queries = []
    for first in range(0, len(shifts), 2):
        matrix = jnp.concatenate([w[:WIDTH] for w in weights[first : first + 2]], axis=1)
        queries.append(
            jnp.concatenate(
                [
                    jnp.dot(rows[...], matrix, preferred_element_type=jnp.float32).astype(jnp.bfloat16)
                    for rows in (own_ref, other_ref)
                ],
                axis=0,
            )
        )

    lowest = jnp.minimum(row_docs[0, 0], row_docs[ROWS, 0])
    highest = jnp.maximum(row_docs[ROWS - 1, 0], row_docs[PAIR - 1, 0])

    def reached(i):
        first = jnp.minimum(key_docs[0, i * PAIR], key_docs[0, i * PAIR + ROWS])
        last = jnp.maximum(key_docs[0, i * PAIR + ROWS - 1], key_docs[0, i * PAIR + PAIR - 1])
        return jnp.logical_and(first <= highest, last >= lowest)

    after, before = reached(3), reached(4)
    cases = (
        (jnp.logical_not(jnp.logical_or(after, before)), (0, 1, 2)),
        (jnp.logical_and(after, jnp.logical_not(before)), (0, 1, 2, 3)),
        (jnp.logical_and(before, jnp.logical_not(after)), (0, 1, 2, 4)),
        (jnp.logical_and(after, before), (0, 1, 2, 3, 4)),
    )
    for case, blocks in cases:

        @pl.when(case)
        def _(blocks=blocks):
            for n, shift in enumerate(shifts):
                color = (2 * x + 3 * y + z + shift) % 8
                slot = 0
                for k in range(8):
                    slot = slot + jnp.where(color == k, jnp.where(c == 0, ORDER[0][k], ORDER[1][k]), 0)
                half = queries[n // 2][:, n % 2 * HEAD_SIZE : (n % 2 + 1) * HEAD_SIZE]
                result = attend(half, kv, bases, docs, key_docs, blocks)
                columns = pl.ds(pl.multiple_of(slot * HEAD_SIZE, HEAD_SIZE), HEAD_SIZE)
                keep_ref[:, columns] = result[:ROWS]
                send_ref[:, columns] = result[ROWS:]


def some_heads(arrivals, own, other, kv, row_docs, key_docs, keep, send):
    inputs = [own, other, *(w for _, w in arrivals), *kv, row_docs, key_docs, keep, send]
    bases = [array.shape[0] - 2 * PAIR for array in kv]
    shape = jax.ShapeDtypeStruct(keep.shape, keep.dtype)
    return pl.pallas_call(
        functools.partial(heads_kernel, tuple(shift for shift, _ in arrivals), bases),
        in_specs=[VMEM] * len(inputs),
        out_specs=[VMEM, VMEM],
        out_shape=[shape, shape],
        input_output_aliases={len(inputs) - 2: 0, len(inputs) - 1: 1},
        compiler_params=pltpu.CompilerParams(vmem_limit_bytes=16 * 2**20),
        cost_estimate=pl.CostEstimate(flops=2**28, bytes_accessed=2**21, transcendentals=2**18),
    )(*inputs)


def put_kernel(side, value_ref, *refs):
    out_ref, sem = refs[-2:]
    y, x, z, c = place()
    core = c if side == 0 else 1 - c
    columns = pl.ds(pl.multiple_of(core * HALF, HALF), HALF)
    copy = pltpu.make_async_copy(value_ref, out_ref.at[:, columns], sem)
    copy.start()
    copy.wait()


def put(side, value, result=None):
    inputs = [value] if result is None else [value, result]
    return pl.pallas_call(
        functools.partial(put_kernel, side),
        in_specs=[VMEM, HBM][: len(inputs)],
        out_specs=HBM,
        out_shape=jax.ShapeDtypeStruct((ROWS, 2 * HALF), value.dtype),
        scratch_shapes=[pltpu.SemaphoreType.DMA],
        input_output_aliases={} if result is None else {1: 0},
        compiler_params=pltpu.CompilerParams(vmem_limit_bytes=2**20),
        cost_estimate=pl.CostEstimate(flops=2**24, bytes_accessed=2**18, transcendentals=0),
    )(*inputs)


def body(tokens, query_weight, key_matrix, value_matrix, doc_lengths):
    weight = lax.ppermute(query_weight, AXES, first_moves())
    own, key_mine, value_mine, kv, row_docs, key_docs = own_kv(doc_lengths, tokens, key_matrix, value_matrix)
    other = swap_cores(tokens)
    kv = other_kv(other, key_mine, value_mine, kv)
    near = [lax.ppermute(kv, AXES, moves(lambda c, d=d: (0, 0, d))) for d in (1, -1)]

    weight = gate(weight, kv)
    right = lax.ppermute(weight, AXES, moves(lambda c: (0, 1, 0)))
    left = lax.ppermute(weight, AXES, moves(lambda c: (0, -1, 0)))
    down, up = pack(weight, *near)
    above = lax.ppermute(down, AXES, moves(lambda c: (0, 0, 1)))
    below = lax.ppermute(up, AXES, moves(lambda c: (0, 0, -1)))
    front = lax.ppermute(weight, AXES, moves(lambda c: (1, 0, 0)))
    back = lax.ppermute(weight, AXES, moves(lambda c: (-1, 0, 0)))
    across = lax.ppermute(choose(right, left), AXES, moves(lambda c: (0, 1, 0) if c == 0 else (0, -1, 0)))
    arrivals = [(0, weight), (2, right), (-2, left), (1, above), (-1, below), (3, front), (-3, back), (4, across)]
    kv_all = [kv, *near, above, below]

    keep = jnp.zeros((ROWS, HALF), jnp.bfloat16)
    send = jnp.zeros((ROWS, HALF), jnp.bfloat16)
    for some in (arrivals[:4], arrivals[4:6], arrivals[6:]):
        keep, send = some_heads(some, own, other, kv_all, row_docs, key_docs, keep, send)
    return put(1, swap_cores(send), put(0, keep))


def solution(mesh):
    in_specs = (P(("dp", "ctx"), None), P(None, "ctx"), P(), P(), P("dp"))
    out_specs = P(("dp", "ctx"), None)
    return jax.shard_map(body, mesh=mesh, in_specs=in_specs, out_specs=out_specs, check_vma=False)
```

```python
import functools
import math

import jax
import jax.numpy as jnp
from jax import lax
from jax.experimental import pallas as pl
from jax.experimental.pallas import tpu as pltpu
from jax.sharding import PartitionSpec as P

HEAD_SIZE = 128
WIDTH = 2048
ROWS = 128
PAIR = 2 * ROWS
HALF = 8 * HEAD_SIZE
NEG = -1e30

YS, XS, ZS, CORES = 8, 4, 8, 2
AXES = ("dp", "ctx")
ORDER = ((5, 3, 1, 7, 4, 2, 0, 6), (7, 3, 0, 6, 2, 4, 1, 5))
AROUND = (0, 1, -1, 2, -2)
VMEM = pl.BlockSpec(memory_space=pltpu.VMEM)
HBM = pl.BlockSpec(memory_space=pltpu.HBM)


def flat(y, x, z, c):
    return (((y % YS) * XS + x % XS) * ZS + z % ZS) * CORES + c


def everyone():
    return [(y, x, z, c) for y in range(YS) for x in range(XS) for z in range(ZS) for c in range(CORES)]


def first_moves():
    pairs = []
    for y, x, z, c in everyone():
        head = 8 * c + ORDER[c][(2 * x + 3 * y + z) % 8]
        pairs.append((flat(y, x, head // 2, head % 2), flat(y, x, z, c)))
    return pairs


def moves(step):
    pairs = []
    for y, x, z, c in everyone():
        dy, dx, dz = step(c)
        pairs.append((flat(y + dy, x + dx, z + dz, c), flat(y, x, z, c)))
    return pairs


def swap_cores(value):
    return lax.ppermute(value, AXES, [(flat(y, x, z, 1 - c), flat(y, x, z, c)) for y, x, z, c in everyone()])


def place():
    dp, ctx = lax.axis_index("dp"), lax.axis_index("ctx")
    return dp // XS, dp % XS, ctx // CORES, ctx % CORES


def kv_rows(rows, key_ref, value_ref, kv_ref, first):
    for base, matrix in ((0, key_ref), (PAIR, value_ref)):
        kv_ref[base + first : base + first + ROWS] = jnp.dot(
            rows[...], matrix[...], preferred_element_type=jnp.float32
        ).astype(jnp.bfloat16)


def own_kv_kernel(
    lengths_hbm, own_hbm, key_hbm, value_hbm, own_ref, key_ref, value_ref, kv_ref, row_docs_ref, key_docs_ref, lengths, sems
):
    y, x, z, c = place()
    mine = pl.ds(pl.multiple_of(c * HEAD_SIZE, HEAD_SIZE), HEAD_SIZE)
    copies = [
        pltpu.make_async_copy(own_hbm, own_ref, sems.at[0]),
        pltpu.make_async_copy(key_hbm.at[:, mine], key_ref, sems.at[1]),
        pltpu.make_async_copy(value_hbm.at[:, mine], value_ref, sems.at[2]),
        pltpu.make_async_copy(lengths_hbm, lengths, sems.at[3]),
    ]
    for copy in copies:
        copy.start()

    def positions(shape, axis, block):
        row = lax.broadcasted_iota(jnp.int32, shape, axis)
        return jnp.where(row < ROWS, row + ROWS * c, row - ROWS * c) + PAIR * block

    def docs(place_in_group):
        end = 0
        total = jnp.zeros(place_in_group.shape, jnp.int32)
        for e in range(16):
            end = end + lengths[e]
            total = total + (place_in_group >= end).astype(jnp.int32)
        return total

    copies[3].wait()
    row_docs_ref[...] = docs(positions((PAIR, 1), 0, z))
    for i, step in enumerate(AROUND):
        key_docs_ref[:, i * PAIR : (i + 1) * PAIR] = docs(positions((1, PAIR), 1, (z + step + ZS) % ZS))
    for copy in copies[:3]:
        copy.wait()
    kv_rows(own_ref, key_ref, value_ref, kv_ref, 0)


def own_kv(lengths, own, key_matrix, value_matrix):
    kind = jnp.bfloat16
    return pl.pallas_call(
        own_kv_kernel,
        in_specs=[HBM] * 4,
        out_specs=[VMEM] * 6,
        out_shape=[
            jax.ShapeDtypeStruct((ROWS, WIDTH), kind),
            jax.ShapeDtypeStruct((WIDTH, HEAD_SIZE), kind),
            jax.ShapeDtypeStruct((WIDTH, HEAD_SIZE), kind),
            jax.ShapeDtypeStruct((2 * PAIR, HEAD_SIZE), kind),
            jax.ShapeDtypeStruct((PAIR, 1), jnp.int32),
            jax.ShapeDtypeStruct((1, len(AROUND) * PAIR), jnp.int32),
        ],
        scratch_shapes=[pltpu.SMEM((16,), jnp.int32), pltpu.SemaphoreType.DMA((4,))],
        compiler_params=pltpu.CompilerParams(vmem_limit_bytes=52 * 2**20),
        cost_estimate=pl.CostEstimate(flops=2**27, bytes_accessed=2**21, transcendentals=0),
    )(lengths, own, key_matrix, value_matrix)


def other_kv_kernel(other_ref, key_ref, value_ref, held_ref, kv_ref):
    kv_rows(other_ref, key_ref, value_ref, kv_ref, ROWS)


def other_kv(other, key_mine, value_mine, kv):
    return pl.pallas_call(
        other_kv_kernel,
        in_specs=[VMEM] * 4,
        out_specs=VMEM,
        out_shape=jax.ShapeDtypeStruct(kv.shape, kv.dtype),
        input_output_aliases={3: 0},
        compiler_params=pltpu.CompilerParams(vmem_limit_bytes=8 * 2**20),
        cost_estimate=pl.CostEstimate(flops=2**27, bytes_accessed=2**21, transcendentals=0),
    )(other, key_mine, value_mine, kv)


def gate_kernel(*refs):
    pass


def gate(value, *after):
    return pl.pallas_call(
        gate_kernel,
        in_specs=[VMEM] * (1 + len(after)),
        out_specs=VMEM,
        out_shape=jax.ShapeDtypeStruct(value.shape, value.dtype),
        input_output_aliases={0: 0},
        compiler_params=pltpu.CompilerParams(vmem_limit_bytes=2**20),
    )(value, *after)


def pack_kernel(weight_ref, above_ref, below_ref, down_ref, up_ref):
    down_ref[:WIDTH] = weight_ref[...]
    down_ref[WIDTH:] = above_ref[...]
    up_ref[:WIDTH] = weight_ref[...]
    up_ref[WIDTH:] = below_ref[...]


def pack(weight, above, below):
    packed = jax.ShapeDtypeStruct((weight.shape[0] + above.shape[0], HEAD_SIZE), weight.dtype)
    return pl.pallas_call(
        pack_kernel,
        in_specs=[VMEM] * 3,
        out_specs=[VMEM] * 2,
        out_shape=[packed, packed],
        compiler_params=pltpu.CompilerParams(vmem_limit_bytes=4 * 2**20),
        cost_estimate=pl.CostEstimate(flops=2**32, bytes_accessed=2**21, transcendentals=0),
    )(weight, above, below)


def choose_kernel(first_ref, second_ref, out_ref):
    y, x, z, c = place()

    @pl.when(c == 0)
    def _():
        out_ref[...] = first_ref[...]

    @pl.when(c == 1)
    def _():
        out_ref[...] = second_ref[...]


def choose(first, second):
    return pl.pallas_call(
        choose_kernel,
        in_specs=[VMEM] * 2,
        out_specs=VMEM,
        out_shape=jax.ShapeDtypeStruct(first.shape, first.dtype),
        compiler_params=pltpu.CompilerParams(vmem_limit_bytes=4 * 2**20),
    )(first, second)


def attend(queries, kv, bases, docs, key_docs, blocks):
    factor = math.log2(math.e) / math.sqrt(HEAD_SIZE)
    scores = {}
    for i in blocks:
        product = lax.dot_general(
            queries, kv[i][bases[i] : bases[i] + PAIR], (((1,), (1,)), ((), ())), preferred_element_type=jnp.float32
        )
        allowed = docs == key_docs[:, i * PAIR : (i + 1) * PAIR]
        scores[i] = jnp.where(allowed, product, NEG)
    highest = functools.reduce(jnp.maximum, [jnp.max(s, axis=1, keepdims=True) for s in scores.values()])
    summed, mixed = 0.0, 0.0
    for i in blocks:
        part = jnp.exp2((scores[i] - highest) * factor)
        summed = summed + jnp.sum(part, axis=1, keepdims=True)
        mixed = mixed + jnp.dot(
            part.astype(jnp.bfloat16), kv[i][bases[i] + PAIR : bases[i] + 2 * PAIR], preferred_element_type=jnp.float32
        )
    return (mixed / summed).astype(jnp.bfloat16)


def heads_kernel(shifts, bases, own_ref, other_ref, *refs):
    weights, refs = refs[: len(shifts)], refs[len(shifts) :]
    kv, (row_docs, key_docs, _, _, keep_ref, send_ref) = refs[:5], refs[5:]
    y, x, z, c = place()
    docs = row_docs[...]
    queries = []
    for first in range(0, len(shifts), 2):
        matrix = jnp.concatenate([w[:WIDTH] for w in weights[first : first + 2]], axis=1)
        queries.append(
            jnp.concatenate(
                [
                    jnp.dot(rows[...], matrix, preferred_element_type=jnp.float32).astype(jnp.bfloat16)
                    for rows in (own_ref, other_ref)
                ],
                axis=0,
            )
        )

    lowest = jnp.minimum(row_docs[0, 0], row_docs[ROWS, 0])
    highest = jnp.maximum(row_docs[ROWS - 1, 0], row_docs[PAIR - 1, 0])

    def reached(i):
        first = jnp.minimum(key_docs[0, i * PAIR], key_docs[0, i * PAIR + ROWS])
        last = jnp.maximum(key_docs[0, i * PAIR + ROWS - 1], key_docs[0, i * PAIR + PAIR - 1])
        return jnp.logical_and(first <= highest, last >= lowest)

    after, before = reached(3), reached(4)
    cases = (
        (jnp.logical_not(jnp.logical_or(after, before)), (0, 1, 2)),
        (jnp.logical_and(after, jnp.logical_not(before)), (0, 1, 2, 3)),
        (jnp.logical_and(before, jnp.logical_not(after)), (0, 1, 2, 4)),
        (jnp.logical_and(after, before), (0, 1, 2, 3, 4)),
    )
    for case, blocks in cases:

        @pl.when(case)
        def _(blocks=blocks):
            for n, shift in enumerate(shifts):
                color = (2 * x + 3 * y + z + shift) % 8
                slot = 0
                for k in range(8):
                    slot = slot + jnp.where(color == k, jnp.where(c == 0, ORDER[0][k], ORDER[1][k]), 0)
                half = queries[n // 2][:, n % 2 * HEAD_SIZE : (n % 2 + 1) * HEAD_SIZE]
                result = attend(half, kv, bases, docs, key_docs, blocks)
                columns = pl.ds(pl.multiple_of(slot * HEAD_SIZE, HEAD_SIZE), HEAD_SIZE)
                keep_ref[:, columns] = result[:ROWS]
                send_ref[:, columns] = result[ROWS:]


def some_heads(arrivals, own, other, kv, row_docs, key_docs, keep, send):
    inputs = [own, other, *(w for _, w in arrivals), *kv, row_docs, key_docs, keep, send]
    bases = [array.shape[0] - 2 * PAIR for array in kv]
    shape = jax.ShapeDtypeStruct(keep.shape, keep.dtype)
    return pl.pallas_call(
        functools.partial(heads_kernel, tuple(shift for shift, _ in arrivals), bases),
        in_specs=[VMEM] * len(inputs),
        out_specs=[VMEM, VMEM],
        out_shape=[shape, shape],
        input_output_aliases={len(inputs) - 2: 0, len(inputs) - 1: 1},
        compiler_params=pltpu.CompilerParams(vmem_limit_bytes=16 * 2**20),
        cost_estimate=pl.CostEstimate(flops=2**28, bytes_accessed=2**21, transcendentals=2**18),
    )(*inputs)


def put_kernel(side, value_ref, *refs):
    out_ref, sem = refs[-2:]
    y, x, z, c = place()
    core = c if side == 0 else 1 - c
    columns = pl.ds(pl.multiple_of(core * HALF, HALF), HALF)
    copy = pltpu.make_async_copy(value_ref, out_ref.at[:, columns], sem)
    copy.start()
    copy.wait()


def put(side, value, result=None):
    inputs = [value] if result is None else [value, result]
    return pl.pallas_call(
        functools.partial(put_kernel, side),
        in_specs=[VMEM, HBM][: len(inputs)],
        out_specs=HBM,
        out_shape=jax.ShapeDtypeStruct((ROWS, 2 * HALF), value.dtype),
        scratch_shapes=[pltpu.SemaphoreType.DMA],
        input_output_aliases={} if result is None else {1: 0},
        compiler_params=pltpu.CompilerParams(vmem_limit_bytes=2**20),
        cost_estimate=pl.CostEstimate(flops=2**24, bytes_accessed=2**18, transcendentals=0),
    )(*inputs)


def body(tokens, query_weight, key_matrix, value_matrix, doc_lengths):
    weight = lax.ppermute(query_weight, AXES, first_moves())
    own, key_mine, value_mine, kv, row_docs, key_docs = own_kv(doc_lengths, tokens, key_matrix, value_matrix)
    other = swap_cores(tokens)
    kv = other_kv(other, key_mine, value_mine, kv)
    near = [lax.ppermute(kv, AXES, moves(lambda c, d=d: (0, 0, d))) for d in (1, -1)]

    weight = gate(weight, kv)
    right = lax.ppermute(weight, AXES, moves(lambda c: (0, 1, 0)))
    left = lax.ppermute(weight, AXES, moves(lambda c: (0, -1, 0)))
    down, up = pack(weight, *near)
    above = lax.ppermute(down, AXES, moves(lambda c: (0, 0, 1)))
    below = lax.ppermute(up, AXES, moves(lambda c: (0, 0, -1)))
    front = lax.ppermute(weight, AXES, moves(lambda c: (1, 0, 0)))
    back = lax.ppermute(weight, AXES, moves(lambda c: (-1, 0, 0)))
    across = lax.ppermute(choose(right, left), AXES, moves(lambda c: (0, 1, 0) if c == 0 else (0, -1, 0)))
    arrivals = [(0, weight), (2, right), (-2, left), (1, above), (-1, below), (3, front), (-3, back), (4, across)]
    kv_all = [kv, *near, above, below]

    keep = jnp.zeros((ROWS, HALF), jnp.bfloat16)
    send = jnp.zeros((ROWS, HALF), jnp.bfloat16)
    for some in (arrivals[:4], arrivals[4:6], arrivals[6:]):
        keep, send = some_heads(some, own, other, kv_all, row_docs, key_docs, keep, send)
    return put(1, swap_cores(send), put(0, keep))


def solution(mesh):
    in_specs = (P(("dp", "ctx"), None), P(None, "ctx"), P(), P(), P("dp"))
    out_specs = P(("dp", "ctx"), None)
    return jax.shard_map(body, mesh=mesh, in_specs=in_specs, out_specs=out_specs, check_vma=False)
```
